128 devices in a mesh: seg: 8 (over z, y_lo), slab: 16 (over x, y_hi, core).
Axes of the slice: x: 4, y: 4 (y_hi: 2, y_lo: 2; y = y_hi * 2 + y_lo), z: 4, core: 2. Of those that a mesh axis runs over, the one named last changes fastest.
Arguments:
- state: float32 [8, 2, 4, 64, 64, 128], P('seg', None, None, 'slab'), may hold values from -6 to 6
- base_flow: float32 [8, 3, 64, 64, 128], P('seg', None, 'slab'), may hold values from -0.6 to 1.7, as said below
Outputs:
- advanced: float32 [8, 2, 4, 64, 64, 128], P('seg', None, None, 'slab')
- residual: float32 [8, 2, 4, 64, 64, 128], P('seg', None, None, 'slab')
The draws below stay inside these ranges and needn't reach their ends.
Inputs may be any that keep to these rules, and one draw needn't show every extreme that they name: `base_flow`: component 0 of the base flow lies between 1.3 and 1.7 in every cell; components 1 and 2 lie between -0.6 and 1.4.
All inputs are finite; a program needn't handle non-finite values.
Results may differ from the reference program's by a relative error of at most 0.00002.
Values sent between devices are 32-bit elements; how exact they have to be, the bound alone decides.
No kernel may reach another device: no remote copies, remote signals or barrier semaphores. Data moves between devices by JAX's collectives and lax.ppermute only.
A program may use at most 128 MiB of HBM per device.

```python
import jax
import jax.numpy as jnp
from jax import lax

NY = 64
NZ = 128
VECS = 2
SEGS = 8
NX = 64


def draw_base_flow(key, part):
    key = jax.random.fold_in(key, 11)
    key_stream, key_cross = jax.random.split(key)
    stream_draw = jax.random.uniform(key_stream, (SEGS, 1, NX, NY, NZ), jnp.float32)
    cross_draw = jax.random.uniform(key_cross, (SEGS, 2, NX, NY, NZ), jnp.float32)
    stream = 1.3 + 0.4 * stream_draw
    cross = -0.6 + 2.0 * cross_draw
    return jnp.concatenate([stream, cross], axis=1)


def steps_of(key, dims, shards, least, largest):
    loudness, own = 1.0, jax.random.fold_in(key, 6)
    for dim, blocks in shards:
        draws = jnp.exp(jax.random.uniform(jax.random.fold_in(own, dim), (blocks,), jnp.float32, least / len(shards), largest / len(shards)))
        loudness = loudness * jnp.repeat(draws, dims[dim] // blocks).reshape([-1 if axis == dim else 1 for axis in range(len(dims))])
    return loudness


def gaussian(stream_key, extent, scale, bound, cuts=(), held_as=jnp.bfloat16):
    values = jax.random.normal(stream_key, extent, jnp.float32) * scale
    if len(cuts) > 0:
        values = steps_of(stream_key, extent, cuts, -0.22, 0.18) * values
    return jnp.clip(values, min=-bound, max=bound).astype(held_as)


def setup_inputs(seed: int = 0) -> dict:
    key_of = jax.random.split(jax.random.key(seed), 3)
    state = gaussian(key_of[0], (SEGS, VECS, 4, NX, NY, NZ), 1.0, 6.0, ((0, 8), (3, 16)), jnp.float32)
    base_flow = draw_base_flow(jax.random.fold_in(key_of[2], 71), 0)
    return {"state": state, "base_flow": base_flow}


time_step = 0.4
viscosity = 0.067
sound_sq = 1.0


def x_inner(f):
    return f[..., 1:-1, :, :]


def y_padded(f):
    widths = [(0, 0)] * (f.ndim - 2) + [(1, 1), (0, 0)]
    return jnp.pad(f, widths)


def diff_x(f):
    return 0.5 * (f[..., 2:, :, :] - f[..., :-2, :, :])


def diff_y(f):
    padded = y_padded(f)
    return 0.5 * (padded[..., 2:, :] - padded[..., :-2, :])


def diff_z(f):
    return 0.5 * (jnp.roll(f, -1, -1) - jnp.roll(f, 1, -1))


def laplace(f):
    inner = x_inner(f)
    padded = y_padded(inner)
    total = f[..., 2:, :, :] + f[..., :-2, :, :]
    total = total + padded[..., 2:, :] + padded[..., :-2, :]
    total = total + jnp.roll(inner, -1, -1) + jnp.roll(inner, 1, -1)
    return total - 6.0 * inner


def rates(block, flow):
    velo = block[..., 0:3, :, :, :]
    press = block[..., 3, :, :, :]
    velo_in = x_inner(velo)
    press_in = x_inner(press)
    flow_in = x_inner(flow)
    advect = flow_in[..., 0:1, :, :, :] * diff_x(velo)
    advect = advect + flow_in[..., 1:2, :, :, :] * diff_y(velo_in)
    advect = advect + flow_in[..., 2:3, :, :, :] * diff_z(velo_in)
    react = velo_in[..., 0:1, :, :, :] * diff_x(flow)
    react = react + velo_in[..., 1:2, :, :, :] * diff_y(flow_in)
    react = react + velo_in[..., 2:3, :, :, :] * diff_z(flow_in)
    grad_p = jnp.stack([diff_x(press), diff_y(press_in), diff_z(press_in)], axis=-4)
    dvelo = -advect - react - grad_p + viscosity * laplace(velo)
    diverg = diff_x(velo[..., 0, :, :, :]) + diff_y(velo_in[..., 1, :, :, :]) + diff_z(velo_in[..., 2, :, :, :])
    dpress = -sound_sq * diverg
    return jnp.concatenate([dvelo, dpress[..., None, :, :, :]], axis=-4)


def x_padded(f):
    widths = [(0, 0)] * (f.ndim - 3) + [(1, 1), (0, 0), (0, 0)]
    return jnp.pad(f, widths)


def runge_kutta(pair):
    block, flow = pair
    flow_pad = x_padded(flow)
    section_one = rates(x_padded(block), flow_pad)
    section_two = rates(x_padded(block + (time_step / 2) * section_one), flow_pad)
    section_three = rates(x_padded(block + (time_step / 2) * section_two), flow_pad)
    section_four = rates(x_padded(block + time_step * section_three), flow_pad)
    return block + (time_step / 6) * (((section_one + 2.0 * section_two) + 2.0 * section_three) + section_four)


def reference(state, base_flow):
    advanced = lax.map(runge_kutta, (state, base_flow))
    residual = state - jnp.roll(advanced, 1, axis=0)
    return advanced, residual
```

```python
import functools

import jax
import jax.numpy as jnp
from jax import lax
from jax.experimental import pallas as pl
from jax.experimental.pallas import tpu as pltpu
from jax.sharding import PartitionSpec as P

time_step = 0.4
viscosity = 0.067
sound_sq = 1.0

OWN = 4
HALO = 2
WIDE = OWN + 2 * HALO
TILE = 8
F32 = jnp.float32


def core():
    return lax.rem(lax.axis_index("slab"), 2)


def at_end():
    slab = lax.axis_index("slab")
    return jnp.logical_or(slab == 0, slab == lax.axis_size("slab") - 1)


def outer_side(width):
    far = core() * (OWN - width)
    return far, (OWN - width) - far


def rows_around(ref, field, plane, row, rows):
    here = ref[field, plane, row : row + TILE, :]
    index = lax.broadcasted_iota(jnp.int32, here.shape, 0)
    if row == 0:
        below = jnp.where(index == 0, 0.0, pltpu.roll(here, 1, 0))
    else:
        below = ref[field, plane, row - 1 : row - 1 + TILE, :]
    if row + TILE == rows:
        above = jnp.where(index == TILE - 1, 0.0, pltpu.roll(here, TILE - 1, 0))
    else:
        above = ref[field, plane, row + 1 : row + 1 + TILE, :]
    return here, below, above


def around(ref, field, plane, row, rows):
    here, y_below, y_above = rows_around(ref, field, plane, row, rows)
    lanes = here.shape[1]
    return (
        here,
        ref[field, plane - 1, row : row + TILE, :],
        ref[field, plane + 1, row : row + TILE, :],
        y_below,
        y_above,
        pltpu.roll(here, 1, 1),
        pltpu.roll(here, lanes - 1, 1),
    )


def tile_rates(q, flow, plane, row, rows):
    fields = [around(q, j, plane, row, rows) for j in range(4)]
    base = [around(flow, j, plane, row, rows) for j in range(3)]
    press = fields[3]
    half = [0.5 * b[0] for b in base]
    lower = [viscosity + h for h in half]
    upper = [viscosity - h for h in half]
    react = [-0.5 * f[0] for f in fields[:3]]
    rates = []
    for j in range(3):
        f, b = fields[j], base[j]
        total = (-6.0 * viscosity) * f[0]
        for i in range(3):
            total = total + lower[i] * f[1 + 2 * i]
            total = total + upper[i] * f[2 + 2 * i]
            total = total + react[i] * (b[2 + 2 * i] - b[1 + 2 * i])
        total = total - 0.5 * (press[2 + 2 * j] - press[1 + 2 * j])
        rates.append(total)
    div = (fields[0][2] - fields[0][1]) + (fields[1][4] - fields[1][3])
    div = div + (fields[2][6] - fields[2][5])
    rates.append((-0.5 * sound_sq) * div)
    return [f[0] for f in fields], rates


def over_tiles(first, last, rows, body):
    @pl.loop(first, last)
    def _(plane):
        for row in range(0, rows, TILE):
            body(plane, row)


def run_copies(copies):
    for copy in copies:
        copy.start()
    for copy in copies:
        copy.wait()


def zero_planes(ref, first, width):
    ref[:, pl.ds(first, width)] = jnp.zeros((ref.shape[0], width) + ref.shape[2:], F32)


def pack_kernel(state, flow, far_a, far_b, near, sems):
    far, close = outer_side(HALO)
    pairs = [
        (flow.at[0, :, pl.ds(far, HALO)], far_a.at[0:3]),
        (state.at[0, 0, :, pl.ds(far, HALO)], far_a.at[3:7]),
        (state.at[0, 1, :, pl.ds(far, HALO)], far_b),
        (flow.at[0, :, pl.ds(close, HALO)], near.at[0:3]),
        (state.at[0, 0, :, pl.ds(close, HALO)], near.at[3:7]),
        (state.at[0, 1, :, pl.ds(close, HALO)], near.at[7:11]),
    ]
    run_copies([pltpu.make_async_copy(a, b, sems.at[i]) for i, (a, b) in enumerate(pairs)])


def first_kernel(vec, far_at, state, flow, near, far_flow, far_q, after, mid, part, far_out, near_out, q, base, second, sems):
    del after
    rows = q.shape[2]
    far, close = core() * (OWN + HALO), (1 - core()) * (OWN + HALO)
    pairs = [
        (state.at[0, vec], q.at[:, HALO : HALO + OWN]),
        (flow.at[0], base.at[:, HALO : HALO + OWN]),
        (near.at[0:3], base.at[:, pl.ds(close, HALO)]),
        (near.at[3 + 4 * vec : 7 + 4 * vec], q.at[:, pl.ds(close, HALO)]),
        (far_flow.at[0:3], base.at[:, pl.ds(far, HALO)]),
        (far_q.at[far_at : far_at + 4], q.at[:, pl.ds(far, HALO)]),
    ]
    run_copies([pltpu.make_async_copy(a, b, sems.at[i]) for i, (a, b) in enumerate(pairs)])

    @pl.when(at_end())
    def _():
        zero_planes(q, far, HALO)
        zero_planes(base, far, HALO)

    def one(plane, row):
        here, rates = tile_rates(q, base, plane, row, rows)
        for j in range(4):
            second[j, plane, row : row + TILE, :] = here[j] + (time_step / 2) * rates[j]

    over_tiles(1, WIDE - 1, rows, one)

    @pl.when(at_end())
    def _():
        zero_planes(second, 1 + core() * (WIDE - 3), 1)

    def two(plane, row):
        here, rates = tile_rates(second, base, plane, row, rows)
        for j in range(4):
            start = q[j, plane, row : row + TILE, :]
            third = start + (time_step / 2) * rates[j]
            mid[j, plane - HALO, row : row + TILE, :] = third
            part[j, plane - HALO, row : row + TILE, :] = (here[j] + 2.0 * third - start) * (1.0 / 3.0)

    over_tiles(HALO, HALO + OWN, rows, two)
    far, close = outer_side(HALO)
    far_out[...] = mid[:, pl.ds(far, HALO)]
    near_out[...] = mid[:, pl.ds(close, HALO)]


def second_kernel(vec, far_at, state, flow, near, far_flow, far_q, mid, part, far_mid, near_mid, after, out, q, base, third, fourth, held, sems):
    del after
    rows = q.shape[2]
    far, close = core() * (OWN + HALO), (1 - core()) * (OWN + HALO)
    pairs = [
        (state.at[0, vec], q.at[:, HALO : HALO + OWN]),
        (flow.at[0], base.at[:, HALO : HALO + OWN]),
        (near.at[0:3], base.at[:, pl.ds(close, HALO)]),
        (near.at[3 + 4 * vec : 7 + 4 * vec], q.at[:, pl.ds(close, HALO)]),
        (far_flow.at[0:3], base.at[:, pl.ds(far, HALO)]),
        (far_q.at[far_at : far_at + 4], q.at[:, pl.ds(far, HALO)]),
        (mid, third.at[:, HALO : HALO + OWN]),
        (near_mid, third.at[:, pl.ds(close, HALO)]),
        (far_mid, third.at[:, pl.ds(far, HALO)]),
        (part, held),
    ]
    run_copies([pltpu.make_async_copy(a, b, sems.at[i]) for i, (a, b) in enumerate(pairs)])

    @pl.when(at_end())
    def _():
        zero_planes(third, far, HALO)
        zero_planes(base, far, HALO)

    def one(plane, row):
        _, rates = tile_rates(third, base, plane, row, rows)
        for j in range(4):
            fourth[j, plane, row : row + TILE, :] = q[j, plane, row : row + TILE, :] + time_step * rates[j]

    over_tiles(1, WIDE - 1, rows, one)

    @pl.when(at_end())
    def _():
        zero_planes(fourth, 1 + core() * (WIDE - 3), 1)

    def two(plane, row):
        here, rates = tile_rates(fourth, base, plane, row, rows)
        for j in range(4):
            total = held[j, plane - HALO, row : row + TILE, :] + (1.0 / 3.0) * here[j]
            out[j, plane - HALO, row : row + TILE, :] = total + (time_step / 6) * rates[j]

    over_tiles(HALO, HALO + OWN, rows, two)


def shards(state, flow):
    rows, lanes = state.shape[-2:]
    slabs, segs = lax.axis_size("slab"), lax.axis_size("seg")
    near_pairs = [(i, i ^ 1) for i in range(slabs)]
    far_pairs = [(i, (i + 1) % slabs if i % 2 else (i - 1) % slabs) for i in range(slabs)]
    seg_pairs = [(i, (i + 1) % segs) for i in range(segs)]

    def planes(fields, count):
        return jax.ShapeDtypeStruct((fields, count, rows, lanes), F32)

    def scratch(fields, count):
        return pltpu.VMEM((fields, count, rows, lanes), F32)

    anywhere = pl.BlockSpec(memory_space=pl.ANY)
    vmem = pl.BlockSpec(memory_space=pltpu.VMEM)
    cost = pl.CostEstimate(flops=30_000_000, bytes_accessed=6_000_000, transcendentals=0)
    params = pltpu.CompilerParams(vmem_limit_bytes=16 * 1024 * 1024)

    far_a, far_b, near = pl.pallas_call(
        pack_kernel,
        out_shape=(planes(7, HALO), planes(4, HALO), planes(11, HALO)),
        in_specs=[anywhere] * 2,
        out_specs=(vmem,) * 3,
        scratch_shapes=[pltpu.SemaphoreType.DMA((6,))],
        compiler_params=params,
        name="pack",
    )(state, flow)
    far_a = lax.ppermute(far_a, "slab", far_pairs)
    near = lax.ppermute(near, "slab", near_pairs)
    far_b = lax.ppermute(far_b, "slab", far_pairs)

    def first(vec, after):
        far_at, far_q = (3, far_a) if vec == 0 else (0, far_b)
        return pl.pallas_call(
            functools.partial(first_kernel, vec, far_at),
            out_shape=(planes(4, OWN), planes(4, OWN), planes(4, HALO), planes(4, HALO)),
            in_specs=[anywhere] * 6,
            out_specs=(vmem,) * 4,
            scratch_shapes=[scratch(4, WIDE), scratch(3, WIDE), scratch(4, WIDE), pltpu.SemaphoreType.DMA((6,))],
            compiler_params=params,
            cost_estimate=cost,
            name=f"first_{vec}",
        )(state, flow, near, far_a, far_q, after)

    def second(vec, mid, part, far_mid, near_mid, after):
        far_at, far_q = (3, far_a) if vec == 0 else (0, far_b)
        return pl.pallas_call(
            functools.partial(second_kernel, vec, far_at),
            out_shape=planes(4, OWN),
            in_specs=[anywhere] * 10,
            out_specs=vmem,
            scratch_shapes=[
                scratch(4, WIDE),
                scratch(3, WIDE),
                scratch(4, WIDE),
                scratch(4, WIDE),
                scratch(4, OWN),
                pltpu.SemaphoreType.DMA((10,)),
            ],
            compiler_params=params,
            cost_estimate=cost,
            name=f"second_{vec}",
        )(state, flow, near, far_a, far_q, mid, part, far_mid, near_mid, after)

    mid0, part0, far0, near0 = first(0, far_a)
    far0 = lax.ppermute(far0, "slab", far_pairs)
    near0 = lax.ppermute(near0, "slab", near_pairs)
    mid1, part1, far1, near1 = first(1, mid0)
    far1 = lax.ppermute(far1, "slab", far_pairs)
    near1 = lax.ppermute(near1, "slab", near_pairs)
    out0 = second(0, mid0, part0, far0, near0, mid1)
    prev0 = lax.ppermute(out0, "seg", seg_pairs)
    out1 = second(1, mid1, part1, far1, near1, out0)
    prev1 = lax.ppermute(out1, "seg", seg_pairs)
    advanced = jnp.stack([out0, out1])[None]
    residual = jnp.stack([state[0, 0] - prev0, state[0, 1] - prev1])[None]
    return advanced, residual


def solution(mesh):
    return jax.shard_map(
        shards,
        mesh=mesh,
        in_specs=(P("seg", None, None, "slab", None, None), P("seg", None, "slab", None, None)),
        out_specs=(
            P("seg", None, None, "slab", None, None),
            P("seg", None, None, "slab", None, None),
        ),
        check_vma=False,
    )
```

```python
import functools

import jax
import jax.numpy as jnp
from jax import lax
from jax.experimental import pallas as pl
from jax.experimental.pallas import tpu as pltpu
from jax.sharding import PartitionSpec as P

time_step = 0.4
viscosity = 0.067
sound_sq = 1.0

OWN = 4
HALO = 2
WIDE = OWN + 2 * HALO
TILE = 8
F32 = jnp.float32


def core():
    return lax.rem(lax.axis_index("slab"), 2)


def at_end():
    slab = lax.axis_index("slab")
    return jnp.logical_or(slab == 0, slab == lax.axis_size("slab") - 1)


def outer_side(width):
    far = core() * (OWN - width)
    return far, (OWN - width) - far


def rows_around(ref, field, plane, row, rows):
    here = ref[field, plane, row : row + TILE, :]
    index = lax.broadcasted_iota(jnp.int32, here.shape, 0)
    if row == 0:
        below = jnp.where(index == 0, 0.0, pltpu.roll(here, 1, 0))
    else:
        below = ref[field, plane, row - 1 : row - 1 + TILE, :]
    if row + TILE == rows:
        above = jnp.where(index == TILE - 1, 0.0, pltpu.roll(here, TILE - 1, 0))
    else:
        above = ref[field, plane, row + 1 : row + 1 + TILE, :]
    return here, below, above


def around(ref, field, plane, row, rows):
    here, y_below, y_above = rows_around(ref, field, plane, row, rows)
    lanes = here.shape[1]
    return (
        here,
        ref[field, plane - 1, row : row + TILE, :],
        ref[field, plane + 1, row : row + TILE, :],
        y_below,
        y_above,
        pltpu.roll(here, 1, 1),
        pltpu.roll(here, lanes - 1, 1),
    )


def tile_rates(q, flow, plane, row, rows):
    fields = [around(q, j, plane, row, rows) for j in range(4)]
    base = [around(flow, j, plane, row, rows) for j in range(3)]
    press = fields[3]
    half = [0.5 * b[0] for b in base]
    lower = [viscosity + h for h in half]
    upper = [viscosity - h for h in half]
    react = [-0.5 * f[0] for f in fields[:3]]
    rates = []
    for j in range(3):
        f, b = fields[j], base[j]
        total = (-6.0 * viscosity) * f[0]
        for i in range(3):
            total = total + lower[i] * f[1 + 2 * i]
            total = total + upper[i] * f[2 + 2 * i]
            total = total + react[i] * (b[2 + 2 * i] - b[1 + 2 * i])
        total = total - 0.5 * (press[2 + 2 * j] - press[1 + 2 * j])
        rates.append(total)
    div = (fields[0][2] - fields[0][1]) + (fields[1][4] - fields[1][3])
    div = div + (fields[2][6] - fields[2][5])
    rates.append((-0.5 * sound_sq) * div)
    return [f[0] for f in fields], rates


def over_tiles(first, last, rows, body):
    @pl.loop(first, last)
    def _(plane):
        for row in range(0, rows, TILE):
            body(plane, row)


def run_copies(copies):
    for copy in copies:
        copy.start()
    for copy in copies:
        copy.wait()


def zero_planes(ref, first, width):
    ref[:, pl.ds(first, width)] = jnp.zeros((ref.shape[0], width) + ref.shape[2:], F32)


def pack_kernel(state, flow, far_a, near, sems):
    far, close = outer_side(HALO)
    pairs = [
        (flow.at[0, :, pl.ds(far, HALO)], far_a.at[0:3]),
        (state.at[0, 0, :, pl.ds(far, HALO)], far_a.at[3:7]),
        (flow.at[0, :, pl.ds(close, HALO)], near.at[0:3]),
        (state.at[0, 0, :, pl.ds(close, HALO)], near.at[3:7]),
        (state.at[0, 1, :, pl.ds(close, HALO)], near.at[7:11]),
    ]
    run_copies([pltpu.make_async_copy(a, b, sems.at[i]) for i, (a, b) in enumerate(pairs)])


def stage_one(q, base, second, first, count):
    rows = q.shape[2]

    def one(plane, row):
        here, rates = tile_rates(q, base, plane, row, rows)
        for j in range(4):
            second[j, plane, row : row + TILE, :] = here[j] + (time_step / 2) * rates[j]

    over_tiles(first, first + count, rows, one)


def stage_two(q, base, second, mid, part, first, count, shift):
    rows = q.shape[2]

    def two(plane, row):
        here, rates = tile_rates(second, base, plane, row, rows)
        for j in range(4):
            start = q[j, plane, row : row + TILE, :]
            third = start + (time_step / 2) * rates[j]
            mid[j, plane - shift, row : row + TILE, :] = third
            part[j, plane - shift, row : row + TILE, :] = (here[j] + 2.0 * third - start) * (1.0 / 3.0)

    over_tiles(first, first + count, rows, two)


def inner_kernel(vec, state, flow, near, after, second_out, mid, part, *rest):
    del after
    far_out = rest[0] if vec else None
    q, base, second, sems = rest[-4:]
    close = (1 - core()) * (OWN + HALO)
    pairs = [
        (state.at[0, vec], q.at[:, HALO : HALO + OWN]),
        (flow.at[0], base.at[:, HALO : HALO + OWN]),
        (near.at[0:3], base.at[:, pl.ds(close, HALO)]),
        (near.at[3 + 4 * vec : 7 + 4 * vec], q.at[:, pl.ds(close, HALO)]),
    ]
    run_copies([pltpu.make_async_copy(a, b, sems.at[i]) for i, (a, b) in enumerate(pairs)])
    lowest = 3 - 2 * core()
    stage_one(q, base, second, lowest, OWN)
    second_out[...] = second[:, pl.ds(lowest, OWN)]
    stage_two(q, base, second, mid, part, lowest + 1, HALO, lowest + 1)
    if vec:
        far, _ = outer_side(HALO)
        far_out[...] = q[:, pl.ds(HALO + far, HALO)]


def first_kernel(vec, far_at, state, flow, near, far_flow, far_q, second_in, mid_in, part_in, after, mid, part, far_out, q, base, second, sems):
    del after
    far, close = core() * (OWN + HALO), (1 - core()) * (OWN + HALO)
    outer, inner = HALO * core(), HALO * (1 - core())
    pairs = [
        (state.at[0, vec, :, pl.ds(outer, HALO)], q.at[:, pl.ds(HALO + outer, HALO)]),
        (flow.at[0], base.at[:, HALO : HALO + OWN]),
        (far_flow.at[0:3], base.at[:, pl.ds(far, HALO)]),
        (far_q.at[far_at : far_at + 4], q.at[:, pl.ds(far, HALO)]),
        (second_in, second.at[:, pl.ds(3 - 2 * core(), OWN)]),
        (mid_in, mid.at[:, pl.ds(inner, HALO)]),
        (part_in, part.at[:, pl.ds(inner, HALO)]),
    ]
    run_copies([pltpu.make_async_copy(a, b, sems.at[i]) for i, (a, b) in enumerate(pairs)])

    @pl.when(at_end())
    def _():
        zero_planes(q, far, HALO)
        zero_planes(base, far, HALO)

    stage_one(q, base, second, 1 + OWN * core(), HALO)

    @pl.when(at_end())
    def _():
        zero_planes(second, 1 + core() * (WIDE - 3), 1)

    stage_two(q, base, second, mid, part, HALO + outer, HALO, HALO)
    far, _ = outer_side(HALO)
    far_out[...] = mid[:, pl.ds(far, HALO)]


def second_kernel(vec, far_at, state, flow, near, far_flow, far_q, mid, part, far_mid, near_mid, after, out, q, base, third, fourth, held, sems):
    del after
    rows = q.shape[2]
    far, close = core() * (OWN + HALO), (1 - core()) * (OWN + HALO)
    pairs = [
        (state.at[0, vec], q.at[:, HALO : HALO + OWN]),
        (flow.at[0], base.at[:, HALO : HALO + OWN]),
        (near.at[0:3], base.at[:, pl.ds(close, HALO)]),
        (near.at[3 + 4 * vec : 7 + 4 * vec], q.at[:, pl.ds(close, HALO)]),
        (far_flow.at[0:3], base.at[:, pl.ds(far, HALO)]),
        (far_q.at[far_at : far_at + 4], q.at[:, pl.ds(far, HALO)]),
        (mid, third.at[:, HALO : HALO + OWN]),
        (near_mid, third.at[:, pl.ds(close, HALO)]),
        (far_mid, third.at[:, pl.ds(far, HALO)]),
        (part, held),
    ]
    run_copies([pltpu.make_async_copy(a, b, sems.at[i]) for i, (a, b) in enumerate(pairs)])

    @pl.when(at_end())
    def _():
        zero_planes(third, far, HALO)
        zero_planes(base, far, HALO)

    def one(plane, row):
        _, rates = tile_rates(third, base, plane, row, rows)
        for j in range(4):
            fourth[j, plane, row : row + TILE, :] = q[j, plane, row : row + TILE, :] + time_step * rates[j]

    over_tiles(1, WIDE - 1, rows, one)

    @pl.when(at_end())
    def _():
        zero_planes(fourth, 1 + core() * (WIDE - 3), 1)

    def two(plane, row):
        here, rates = tile_rates(fourth, base, plane, row, rows)
        for j in range(4):
            total = held[j, plane - HALO, row : row + TILE, :] + (1.0 / 3.0) * here[j]
            out[j, plane - HALO, row : row + TILE, :] = total + (time_step / 6) * rates[j]

    over_tiles(HALO, HALO + OWN, rows, two)


def shards(state, flow):
    rows, lanes = state.shape[-2:]
    slabs, segs = lax.axis_size("slab"), lax.axis_size("seg")
    near_pairs = [(i, i ^ 1) for i in range(slabs)]
    seg_pairs = [(i, (i + 1) % segs) for i in range(segs)]
    far_pairs = []
    for seg in range(segs):
        for slab in range(slabs):
            if slab in (0, slabs - 1):
                to = (seg ^ 2) * slabs + slab
            else:
                to = seg * slabs + (slab + 1 if slab % 2 else slab - 1)
            far_pairs.append((seg * slabs + slab, to))

    def far_swap(value):
        return lax.ppermute(value, ("seg", "slab"), far_pairs)

    def near_swap(value):
        return lax.ppermute(value, "slab", near_pairs)

    def planes(fields, count):
        return jax.ShapeDtypeStruct((fields, count, rows, lanes), F32)

    def scratch(fields, count):
        return pltpu.VMEM((fields, count, rows, lanes), F32)

    anywhere = pl.BlockSpec(memory_space=pl.ANY)
    vmem = pl.BlockSpec(memory_space=pltpu.VMEM)
    cost = pl.CostEstimate(flops=30_000_000, bytes_accessed=6_000_000, transcendentals=0)
    params = pltpu.CompilerParams(vmem_limit_bytes=16 * 1024 * 1024)

    far_a, near = pl.pallas_call(
        pack_kernel,
        out_shape=(pltpu.VMEM((7, HALO, rows, lanes), F32), pltpu.VMEM((11, HALO, rows, lanes), F32)),
        in_specs=[anywhere] * 2,
        out_specs=(vmem,) * 2,
        scratch_shapes=[pltpu.SemaphoreType.DMA((5,))],
        compiler_params=params,
        name="pack",
    )(pltpu.with_memory_space_constraint(state, pltpu.HBM), pltpu.with_memory_space_constraint(flow, pltpu.HBM))
    far_a = far_swap(far_a)
    near = near_swap(near)

    def inner(vec, after):
        return pl.pallas_call(
            functools.partial(inner_kernel, vec),
            out_shape=(planes(4, OWN), planes(4, HALO), planes(4, HALO)) + (planes(4, HALO),) * vec,
            in_specs=[anywhere] * 4,
            out_specs=(vmem,) * (3 + vec),
            scratch_shapes=[scratch(4, WIDE), scratch(3, WIDE), scratch(4, WIDE), pltpu.SemaphoreType.DMA((4,))],
            compiler_params=params,
            cost_estimate=cost,
            name=f"inner_{vec}",
        )(state, flow, near, after)

    inner0 = inner(0, near)
    *inner1, far_b = inner(1, inner0[1])
    far_b = far_swap(far_b)

    def first(vec, ready, after):
        far_at, far_q = (3, far_a) if vec == 0 else (0, far_b)
        return pl.pallas_call(
            functools.partial(first_kernel, vec, far_at),
            out_shape=(planes(4, OWN), planes(4, OWN), planes(4, HALO)),
            in_specs=[anywhere] * 9,
            out_specs=(vmem,) * 3,
            scratch_shapes=[scratch(4, WIDE), scratch(3, WIDE), scratch(4, WIDE), pltpu.SemaphoreType.DMA((7,))],
            compiler_params=params,
            cost_estimate=cost,
            name=f"first_{vec}",
        )(state, flow, near, far_a, far_q, *ready, after)

    def second(vec, mid, part, far_mid, near_mid, after):
        far_at, far_q = (3, far_a) if vec == 0 else (0, far_b)
        return pl.pallas_call(
            functools.partial(second_kernel, vec, far_at),
            out_shape=planes(4, OWN),
            in_specs=[anywhere] * 10,
            out_specs=vmem,
            scratch_shapes=[
                scratch(4, WIDE),
                scratch(3, WIDE),
                scratch(4, WIDE),
                scratch(4, WIDE),
                scratch(4, OWN),
                pltpu.SemaphoreType.DMA((10,)),
            ],
            compiler_params=params,
            cost_estimate=cost,
            name=f"second_{vec}",
        )(state, flow, near, far_a, far_q, mid, part, far_mid, near_mid, after)

    near0, near1 = near_swap(inner0[1]), near_swap(inner1[1])
    mid0, part0, far0 = first(0, inner0, inner1[1])
    far0 = far_swap(far0)
    mid1, part1, far1 = first(1, inner1, mid0)
    far1 = far_swap(far1)
    out0 = second(0, mid0, part0, far0, near0, mid1)
    prev0 = lax.ppermute(out0, "seg", seg_pairs)
    out1 = second(1, mid1, part1, far1, near1, out0)
    prev1 = lax.ppermute(out1, "seg", seg_pairs)
    advanced = jnp.stack([out0, out1])[None]
    residual = jnp.stack([state[0, 0] - prev0, state[0, 1] - prev1])[None]
    return advanced, residual


def solution(mesh):
    return jax.shard_map(
        shards,
        mesh=mesh,
        in_specs=(P("seg", None, None, "slab", None, None), P("seg", None, "slab", None, None)),
        out_specs=(
            P("seg", None, None, "slab", None, None),
            P("seg", None, None, "slab", None, None),
        ),
        check_vma=False,
    )
```

```python
import functools

import jax
import jax.numpy as jnp
from jax import lax
from jax.experimental import pallas as pl
from jax.experimental.pallas import tpu as pltpu
from jax.sharding import PartitionSpec as P

time_step = 0.4
viscosity = 0.067
sound_sq = 1.0

OWN = 4
HALO = 2
WIDE = OWN + 2 * HALO
TILE = 8
F32 = jnp.float32


def core():
    return lax.rem(lax.axis_index("slab"), 2)


def at_end():
    slab = lax.axis_index("slab")
    return jnp.logical_or(slab == 0, slab == lax.axis_size("slab") - 1)


def outer_side(width):
    far = core() * (OWN - width)
    return far, (OWN - width) - far


def rows_around(ref, field, plane, row, rows):
    here = ref[field, plane, row : row + TILE, :]
    index = lax.broadcasted_iota(jnp.int32, here.shape, 0)
    if row == 0:
        below = jnp.where(index == 0, 0.0, pltpu.roll(here, 1, 0))
    else:
        below = ref[field, plane, row - 1 : row - 1 + TILE, :]
    if row + TILE == rows:
        above = jnp.where(index == TILE - 1, 0.0, pltpu.roll(here, TILE - 1, 0))
    else:
        above = ref[field, plane, row + 1 : row + 1 + TILE, :]
    return here, below, above


def around(ref, field, plane, row, rows):
    here, y_below, y_above = rows_around(ref, field, plane, row, rows)
    lanes = here.shape[1]
    return (
        here,
        ref[field, plane - 1, row : row + TILE, :],
        ref[field, plane + 1, row : row + TILE, :],
        y_below,
        y_above,
        pltpu.roll(here, 1, 1),
        pltpu.roll(here, lanes - 1, 1),
    )


def tile_rates(q, flow, plane, row, rows):
    fields = [around(q, j, plane, row, rows) for j in range(4)]
    base = [around(flow, j, plane, row, rows) for j in range(3)]
    press = fields[3]
    half = [0.5 * b[0] for b in base]
    lower = [viscosity + h for h in half]
    upper = [viscosity - h for h in half]
    react = [-0.5 * f[0] for f in fields[:3]]
    rates = []
    for j in range(3):
        f, b = fields[j], base[j]
        total = (-6.0 * viscosity) * f[0]
        for i in range(3):
            total = total + lower[i] * f[1 + 2 * i]
            total = total + upper[i] * f[2 + 2 * i]
            total = total + react[i] * (b[2 + 2 * i] - b[1 + 2 * i])
        total = total - 0.5 * (press[2 + 2 * j] - press[1 + 2 * j])
        rates.append(total)
    div = (fields[0][2] - fields[0][1]) + (fields[1][4] - fields[1][3])
    div = div + (fields[2][6] - fields[2][5])
    rates.append((-0.5 * sound_sq) * div)
    return [f[0] for f in fields], rates


def finish_halo(q, plane, partial, flow, react, rows, store):
    sign = 1.0 - 2.0 * core().astype(F32)
    edge = plane + 1 - 2 * core()
    for row in range(0, rows, TILE):
        here = [q[j, plane, row : row + TILE, :] for j in range(4)]
        own = [q[j, edge, row : row + TILE, :] for j in range(4)]
        half = (0.5 * sign) * flow[0, plane, row : row + TILE, :]
        factor = viscosity - half
        rates = [partial[j, 0, row : row + TILE, :] + factor * own[j] for j in range(3)]
        rates[0] = rates[0] - (0.5 * sign) * own[3]
        rates.append(partial[3, 0, row : row + TILE, :] - (0.5 * sound_sq * sign) * own[0])
        if react:
            scaled = (0.5 * sign) * here[0]
            for j in range(3):
                rates[j] = rates[j] - scaled * flow[j, edge, row : row + TILE, :]
        store(here, rates, plane, row)


def over_tiles(first, last, rows, body):
    @pl.loop(first, last)
    def _(plane):
        for row in range(0, rows, TILE):
            body(plane, row)


def run_copies(copies):
    for copy in copies:
        copy.start()
    for copy in copies:
        copy.wait()


def zero_planes(ref, first, width):
    ref[:, pl.ds(first, width)] = jnp.zeros((ref.shape[0], width) + ref.shape[2:], F32)


def partial_rates(q, flow, plane, out, first, rows):
    for row in range(0, rows, TILE):
        _, rates = tile_rates(q, flow, plane, row, rows)
        for j in range(4):
            out[first + j, 0, row : row + TILE, :] = rates[j]


def pack_kernel(state, flow, far_a, near, q, base, sems):
    rows = q.shape[2]
    far, close = outer_side(HALO)
    edge, _ = outer_side(1)
    pairs = [
        (flow.at[0, :, pl.ds(far, HALO)], base.at[:, pl.ds(1 - core(), HALO)]),
        (state.at[0, 0, :, pl.ds(far, HALO)], q.at[:, pl.ds(1 - core(), HALO)]),
        (flow.at[0, :, pl.ds(edge, 1)], far_a.at[0:3]),
        (state.at[0, 0, :, pl.ds(edge, 1)], far_a.at[3:7]),
        (flow.at[0, :, pl.ds(close, HALO)], near.at[0:3]),
        (state.at[0, 0, :, pl.ds(close, HALO)], near.at[3:7]),
        (state.at[0, 1, :, pl.ds(close, HALO)], near.at[7:11]),
    ]
    copies = [pltpu.make_async_copy(a, b, sems.at[i]) for i, (a, b) in enumerate(pairs)]
    for copy in copies:
        copy.start()
    zero_planes(q, 2 * core(), 1)
    zero_planes(base, 2 * core(), 1)
    for copy in copies[:2]:
        copy.wait()
    partial_rates(q, base, 1, far_a, 7, rows)
    for copy in copies[2:]:
        copy.wait()


def stage_one(q, base, second, first, count):
    rows = q.shape[2]

    def one(plane, row):
        here, rates = tile_rates(q, base, plane, row, rows)
        for j in range(4):
            second[j, plane, row : row + TILE, :] = here[j] + (time_step / 2) * rates[j]

    over_tiles(first, first + count, rows, one)


def stage_two(q, base, second, mid, part, first, count, shift):
    rows = q.shape[2]

    def two(plane, row):
        here, rates = tile_rates(second, base, plane, row, rows)
        for j in range(4):
            start = q[j, plane, row : row + TILE, :]
            third = start + (time_step / 2) * rates[j]
            mid[j, plane - shift, row : row + TILE, :] = third
            part[j, plane - shift, row : row + TILE, :] = (here[j] + 2.0 * third - start) * (1.0 / 3.0)

    over_tiles(first, first + count, rows, two)


def inner_kernel(vec, state, flow, near, after, second_out, mid, part, *rest):
    del after
    far_out = rest[0] if vec else None
    q, base, second, sems = rest[-4:]
    close = (1 - core()) * (OWN + HALO)
    pairs = [
        (state.at[0, vec], q.at[:, HALO : HALO + OWN]),
        (flow.at[0], base.at[:, HALO : HALO + OWN]),
        (near.at[0:3], base.at[:, pl.ds(close, HALO)]),
        (near.at[3 + 4 * vec : 7 + 4 * vec], q.at[:, pl.ds(close, HALO)]),
    ]
    run_copies([pltpu.make_async_copy(a, b, sems.at[i]) for i, (a, b) in enumerate(pairs)])
    lowest = 3 - 2 * core()
    stage_one(q, base, second, lowest, OWN)
    second_out[...] = second[:, pl.ds(lowest, OWN)]
    stage_two(q, base, second, mid, part, lowest + 1, HALO, lowest + 1)
    if vec:
        edge = HALO + (OWN - 1) * core()
        beyond = HALO - 1 + (OWN + 1) * core()
        zero_planes(q, beyond, 1)
        zero_planes(base, beyond, 1)
        far_out[0:4] = q[:, pl.ds(edge, 1)]
        partial_rates(q, base, edge, far_out, 4, q.shape[2])


def first_kernel(vec, far_at, state, flow, near, far_flow, far_q, second_in, mid_in, part_in, after, mid, part, far_out, q, base, second, third, partial, sems):
    del after
    rows = q.shape[2]
    edge, beyond = HALO + (OWN - 1) * core(), HALO - 1 + (OWN + 1) * core()
    outer, inner = HALO * core(), HALO * (1 - core())
    pairs = [
        (state.at[0, vec, :, pl.ds(outer, HALO)], q.at[:, pl.ds(HALO + outer, HALO)]),
        (flow.at[0], base.at[:, HALO : HALO + OWN]),
        (far_flow.at[0:3], base.at[:, pl.ds(beyond, 1)]),
        (far_q.at[far_at : far_at + 4], q.at[:, pl.ds(beyond, 1)]),
        (far_q.at[far_at + 4 : far_at + 8], partial),
        (second_in, second.at[:, pl.ds(3 - 2 * core(), OWN)]),
        (mid_in, mid.at[:, pl.ds(inner, HALO)]),
        (part_in, part.at[:, pl.ds(inner, HALO)]),
    ]
    run_copies([pltpu.make_async_copy(a, b, sems.at[i]) for i, (a, b) in enumerate(pairs)])

    @pl.when(at_end())
    def _():
        zero_planes(q, beyond, 1)
        zero_planes(base, beyond, 1)

    def one(here, rates, plane, row):
        for j in range(4):
            second[j, plane, row : row + TILE, :] = here[j] + (time_step / 2) * rates[j]

    finish_halo(q, beyond, partial, base, True, rows, one)

    @pl.when(at_end())
    def _():
        zero_planes(second, beyond, 1)

    stage_one(q, base, second, edge, 1)
    stage_two(q, base, second, mid, part, HALO + outer, HALO, HALO)
    third[:, pl.ds(HALO + outer, HALO)] = mid[:, pl.ds(outer, HALO)]
    zero_planes(third, beyond, 1)
    far_out[0:4] = third[:, pl.ds(edge, 1)]
    partial_rates(third, base, edge, far_out, 4, rows)


def second_kernel(vec, far_at, state, flow, near, far_flow, far_q, mid, part, far_mid, near_mid, after, out, q, base, third, fourth, held, partial, sems):
    del after
    rows = q.shape[2]
    beyond, close = HALO - 1 + (OWN + 1) * core(), (1 - core()) * (OWN + HALO)
    pairs = [
        (state.at[0, vec], q.at[:, HALO : HALO + OWN]),
        (flow.at[0], base.at[:, HALO : HALO + OWN]),
        (near.at[0:3], base.at[:, pl.ds(close, HALO)]),
        (near.at[3 + 4 * vec : 7 + 4 * vec], q.at[:, pl.ds(close, HALO)]),
        (far_flow.at[0:3], base.at[:, pl.ds(beyond, 1)]),
        (far_q.at[far_at : far_at + 4], q.at[:, pl.ds(beyond, 1)]),
        (mid, third.at[:, HALO : HALO + OWN]),
        (near_mid, third.at[:, pl.ds(close, HALO)]),
        (far_mid.at[0:4], third.at[:, pl.ds(beyond, 1)]),
        (far_mid.at[4:8], partial),
        (part, held),
    ]
    run_copies([pltpu.make_async_copy(a, b, sems.at[i]) for i, (a, b) in enumerate(pairs)])

    @pl.when(at_end())
    def _():
        zero_planes(third, beyond, 1)
        zero_planes(base, beyond, 1)

    def store(_, rates, plane, row):
        for j in range(4):
            fourth[j, plane, row : row + TILE, :] = q[j, plane, row : row + TILE, :] + time_step * rates[j]

    def one(plane, row):
        store(None, tile_rates(third, base, plane, row, rows)[1], plane, row)

    over_tiles(HALO - core(), HALO - core() + OWN + 1, rows, one)
    finish_halo(third, beyond, partial, base, False, rows, store)

    @pl.when(at_end())
    def _():
        zero_planes(fourth, beyond, 1)

    def two(plane, row):
        here, rates = tile_rates(fourth, base, plane, row, rows)
        for j in range(4):
            total = held[j, plane - HALO, row : row + TILE, :] + (1.0 / 3.0) * here[j]
            out[j, plane - HALO, row : row + TILE, :] = total + (time_step / 6) * rates[j]

    over_tiles(HALO, HALO + OWN, rows, two)


def shards(state, flow):
    rows, lanes = state.shape[-2:]
    slabs, segs = lax.axis_size("slab"), lax.axis_size("seg")
    near_pairs = [(i, i ^ 1) for i in range(slabs)]
    seg_pairs = [(i, (i + 1) % segs) for i in range(segs)]
    far_pairs = []
    for seg in range(segs):
        for slab in range(slabs):
            if slab in (0, slabs - 1):
                to = (seg ^ 2) * slabs + slab
            else:
                to = seg * slabs + (slab + 1 if slab % 2 else slab - 1)
            far_pairs.append((seg * slabs + slab, to))

    def far_swap(value):
        return lax.ppermute(value, ("seg", "slab"), far_pairs)

    def near_swap(value):
        return lax.ppermute(value, "slab", near_pairs)

    def planes(fields, count):
        return jax.ShapeDtypeStruct((fields, count, rows, lanes), F32)

    def scratch(fields, count):
        return pltpu.VMEM((fields, count, rows, lanes), F32)

    anywhere = pl.BlockSpec(memory_space=pl.ANY)
    vmem = pl.BlockSpec(memory_space=pltpu.VMEM)
    cost = pl.CostEstimate(flops=30_000_000, bytes_accessed=6_000_000, transcendentals=0)
    params = pltpu.CompilerParams(vmem_limit_bytes=16 * 1024 * 1024)

    far_a, near = pl.pallas_call(
        pack_kernel,
        out_shape=(pltpu.VMEM((11, 1, rows, lanes), F32), pltpu.VMEM((11, HALO, rows, lanes), F32)),
        in_specs=[anywhere] * 2,
        out_specs=(vmem,) * 2,
        scratch_shapes=[scratch(4, 3), scratch(3, 3), pltpu.SemaphoreType.DMA((7,))],
        compiler_params=params,
        name="pack",
    )(pltpu.with_memory_space_constraint(state, pltpu.HBM), pltpu.with_memory_space_constraint(flow, pltpu.HBM))
    far_a = far_swap(far_a)
    near = near_swap(near)

    def inner(vec, after):
        return pl.pallas_call(
            functools.partial(inner_kernel, vec),
            out_shape=(planes(4, OWN), planes(4, HALO), planes(4, HALO)) + (planes(8, 1),) * vec,
            in_specs=[anywhere] * 4,
            out_specs=(vmem,) * (3 + vec),
            scratch_shapes=[scratch(4, WIDE), scratch(3, WIDE), scratch(4, WIDE), pltpu.SemaphoreType.DMA((4,))],
            compiler_params=params,
            cost_estimate=cost,
            name=f"inner_{vec}",
        )(state, flow, near, after)

    inner0 = inner(0, near)
    *inner1, far_b = inner(1, inner0[1])
    far_b = far_swap(far_b)

    def first(vec, ready, after):
        far_at, far_q = (3, far_a) if vec == 0 else (0, far_b)
        return pl.pallas_call(
            functools.partial(first_kernel, vec, far_at),
            out_shape=(planes(4, OWN), planes(4, OWN), planes(8, 1)),
            in_specs=[anywhere] * 9,
            out_specs=(vmem,) * 3,
            scratch_shapes=[
                scratch(4, WIDE),
                scratch(3, WIDE),
                scratch(4, WIDE),
                scratch(4, WIDE),
                scratch(4, 1),
                pltpu.SemaphoreType.DMA((8,)),
            ],
            compiler_params=params,
            cost_estimate=cost,
            name=f"first_{vec}",
        )(state, flow, near, far_a, far_q, *ready, after)

    def second(vec, mid, part, far_mid, near_mid, after):
        far_at, far_q = (3, far_a) if vec == 0 else (0, far_b)
        return pl.pallas_call(
            functools.partial(second_kernel, vec, far_at),
            out_shape=planes(4, OWN),
            in_specs=[anywhere] * 10,
            out_specs=vmem,
            scratch_shapes=[
                scratch(4, WIDE),
                scratch(3, WIDE),
                scratch(4, WIDE),
                scratch(4, WIDE),
                scratch(4, OWN),
                scratch(4, 1),
                pltpu.SemaphoreType.DMA((11,)),
            ],
            compiler_params=params,
            cost_estimate=cost,
            name=f"second_{vec}",
        )(state, flow, near, far_a, far_q, mid, part, far_mid, near_mid, after)

    near0, near1 = near_swap(inner0[1]), near_swap(inner1[1])
    mid0, part0, far0 = first(0, inner0, inner1[1])
    far0 = far_swap(far0)
    mid1, part1, far1 = first(1, inner1, mid0)
    far1 = far_swap(far1)
    out0 = second(0, mid0, part0, far0, near0, mid1)
    prev0 = lax.ppermute(out0, "seg", seg_pairs)
    out1 = second(1, mid1, part1, far1, near1, out0)
    prev1 = lax.ppermute(out1, "seg", seg_pairs)
    advanced = jnp.stack([out0, out1])[None]
    residual = jnp.stack([state[0, 0] - prev0, state[0, 1] - prev1])[None]
    return advanced, residual


def solution(mesh):
    return jax.shard_map(
        shards,
        mesh=mesh,
        in_specs=(P("seg", None, None, "slab", None, None), P("seg", None, "slab", None, None)),
        out_specs=(
            P("seg", None, None, "slab", None, None),
            P("seg", None, None, "slab", None, None),
        ),
        check_vma=False,
    )
```

```python
import functools

import jax
import jax.numpy as jnp
from jax import lax
from jax.experimental import pallas as pl
from jax.experimental.pallas import tpu as pltpu
from jax.sharding import PartitionSpec as P

time_step = 0.4
viscosity = 0.067
sound_sq = 1.0

OWN = 4
HALO = 2
WIDE = OWN + 2 * HALO
TILE = 8
COEFS = 12
COEF_PLANES = OWN + 1
F32 = jnp.float32


def core():
    return lax.rem(lax.axis_index("slab"), 2)


def at_end():
    slab = lax.axis_index("slab")
    return jnp.logical_or(slab == 0, slab == lax.axis_size("slab") - 1)


def far_edge():
    return HALO + (OWN - 1) * core()


def far_beyond():
    return HALO - 1 + (OWN + 1) * core()


def near_halo():
    return (1 - core()) * (OWN + HALO)


def coef_first():
    return HALO - core()


def far_sign():
    return 1.0 - 2.0 * core().astype(F32)


def tile_of(ref, field, plane, row):
    return ref[field, plane, row : row + TILE, :]


def around(ref, field, plane, row, rows):
    here = tile_of(ref, field, plane, row)
    index = lax.broadcasted_iota(jnp.int32, here.shape, 0)
    if row == 0:
        y_below = jnp.where(index == 0, 0.0, pltpu.roll(here, 1, 0))
    else:
        y_below = ref[field, plane, row - 1 : row - 1 + TILE, :]
    if row + TILE == rows:
        y_above = jnp.where(index == TILE - 1, 0.0, pltpu.roll(here, TILE - 1, 0))
    else:
        y_above = ref[field, plane, row + 1 : row + 1 + TILE, :]
    lanes = here.shape[1]
    return (
        here,
        tile_of(ref, field, plane - 1, row),
        tile_of(ref, field, plane + 1, row),
        y_below,
        y_above,
        pltpu.roll(here, 1, 1),
        pltpu.roll(here, lanes - 1, 1),
    )


def tile_coefs(base, plane, coefs, place, row, rows):
    for j in range(3):
        b = around(base, j, plane, row, rows)
        coefs[j, place, row : row + TILE, :] = 0.5 * b[0]
        for i in range(3):
            coefs[3 + 3 * i + j, place, row : row + TILE, :] = 0.5 * (b[1 + 2 * i] - b[2 + 2 * i])


def tile_rates(q, coefs, plane, place, row, rows, beyond=None):
    fields = [around(q, j, plane, row, rows) for j in range(4)]
    press = fields[3]
    half = [tile_of(coefs, i, place, row) for i in range(3)]
    lower = [viscosity + h for h in half]
    upper = [viscosity - h for h in half]
    rates = []
    for j in range(3):
        f = fields[j]
        total = (-6.0 * viscosity) * f[0] - 0.5 * (press[2 + 2 * j] - press[1 + 2 * j])
        for i in range(3):
            total = total + lower[i] * f[1 + 2 * i]
            total = total + upper[i] * f[2 + 2 * i]
            total = total + fields[i][0] * tile_of(coefs, 3 + 3 * i + j, place, row)
        if beyond is not None:
            total = total + fields[0][0] * tile_of(beyond, j, 0, row)
        rates.append(total)
    div = (fields[0][2] - fields[0][1]) + (fields[1][4] - fields[1][3])
    div = div + (fields[2][6] - fields[2][5])
    rates.append((-0.5 * sound_sq) * div)
    return [f[0] for f in fields], rates


def over_tiles(first, count, rows, body):
    @pl.loop(first, first + count)
    def _(plane):
        for row in range(0, rows, TILE):
            body(plane, row)


def over_rates(q, coefs, first, count, store, beyond=None):
    rows = q.shape[2]

    def body(plane, row):
        here, rates = tile_rates(q, coefs, plane, plane - coef_first(), row, rows, beyond)
        store(here, rates, plane, row)

    over_tiles(first, count, rows, body)


def partial_rates(q, coefs, plane, place, out, first):
    rows = q.shape[2]
    for row in range(0, rows, TILE):
        _, rates = tile_rates(q, coefs, plane, place, row, rows)
        for j in range(4):
            out[first + j, 0, row : row + TILE, :] = rates[j]


def finish_halo(q, partial, coefs, beyond, store):
    sign, plane, edge = far_sign(), far_beyond(), far_edge()
    place = edge - coef_first()
    for row in range(0, q.shape[2], TILE):
        here = [tile_of(q, j, plane, row) for j in range(4)]
        own = [tile_of(q, j, edge, row) for j in range(4)]
        factor = viscosity - tile_of(beyond, 0, 0, row)
        scaled = sign * here[0]
        rates = [
            tile_of(partial, j, 0, row) + factor * own[j] - scaled * tile_of(coefs, j, place, row)
            for j in range(3)
        ]
        rates[0] = rates[0] - (0.5 * sign) * own[3]
        rates.append(tile_of(partial, 3, 0, row) - (0.5 * sound_sq * sign) * own[0])
        store(here, rates, plane, row)


def start_copies(pairs, sems):
    copies = [pltpu.make_async_copy(a, b, sems.at[i]) for i, (a, b) in enumerate(pairs)]
    for copy in copies:
        copy.start()
    return copies


def run_copies(pairs, sems):
    for copy in start_copies(pairs, sems):
        copy.wait()


def zero_planes(ref, first, width):
    ref[:, pl.ds(first, width)] = jnp.zeros((ref.shape[0], width) + ref.shape[2:], F32)


def read_beyond(flow, ref):
    sign = jnp.where(at_end(), 0.0, 0.5 * far_sign())
    ref[...] = sign * flow[...]


def pack_kernel(state, flow, far_a, near, q, base, coefs, sems):
    far, close, edge = core() * (OWN - HALO), (1 - core()) * (OWN - HALO), core() * (OWN - 1)
    pairs = [
        (flow.at[0, :, pl.ds(far, HALO)], base.at[:, pl.ds(1 - core(), HALO)]),
        (state.at[0, 0, :, pl.ds(far, HALO)], q.at[:, pl.ds(1 - core(), HALO)]),
        (flow.at[0, :, pl.ds(edge, 1)], far_a.at[0:3]),
        (state.at[0, 0, :, pl.ds(edge, 1)], far_a.at[3:7]),
        (flow.at[0, :, pl.ds(close, HALO)], near.at[0:3]),
        (state.at[0, 0, :, pl.ds(close, HALO)], near.at[3:7]),
        (state.at[0, 1, :, pl.ds(close, HALO)], near.at[7:11]),
    ]
    copies = start_copies(pairs, sems)
    zero_planes(q, 2 * core(), 1)
    zero_planes(base, 2 * core(), 1)
    copies[0].wait()
    rows = q.shape[2]
    for row in range(0, rows, TILE):
        tile_coefs(base, 1, coefs, 0, row, rows)
    copies[1].wait()
    partial_rates(q, coefs, 1, 0, far_a, 7)
    for copy in copies[2:]:
        copy.wait()


def inner_stages(q, coefs, second, second_out, mid, part):
    lowest = 3 - 2 * core()

    def one(here, rates, plane, row):
        for j in range(4):
            value = here[j] + (time_step / 2) * rates[j]
            second[j, plane, row : row + TILE, :] = value
            second_out[j, plane - lowest, row : row + TILE, :] = value

    over_rates(q, coefs, lowest, OWN, one)
    over_rates(second, coefs, lowest + 1, HALO, second_stage(q, mid, part, lowest + 1))


def second_stage(q, mid, part, shift):
    def two(here, rates, plane, row):
        for j in range(4):
            start = tile_of(q, j, plane, row)
            third = start + (time_step / 2) * rates[j]
            mid[j, plane - shift, row : row + TILE, :] = third
            part[j, plane - shift, row : row + TILE, :] = (here[j] + 2.0 * third - start) * (1.0 / 3.0)

    return two


def inner_0_kernel(state, flow, near, coefs, own0, own1, second_out, mid, part, q, base, second, sems):
    pairs = [
        (flow.at[0], base.at[:, HALO : HALO + OWN]),
        (near.at[0:3], base.at[:, pl.ds(near_halo(), HALO)]),
        (state.at[0, 0], q.at[:, HALO : HALO + OWN]),
        (near.at[3:7], q.at[:, pl.ds(near_halo(), HALO)]),
        (state.at[0, 0], own0),
        (state.at[0, 1], own1),
    ]
    copies = start_copies(pairs, sems)
    zero_planes(base, far_beyond(), 1)
    for copy in copies[:2]:
        copy.wait()
    rows = q.shape[2]
    over_tiles(
        coef_first(),
        COEF_PLANES,
        rows,
        lambda plane, row: tile_coefs(base, plane, coefs, plane - coef_first(), row, rows),
    )
    for copy in copies[2:]:
        copy.wait()
    inner_stages(q, coefs, second, second_out, mid, part)


def inner_1_kernel(own, near, coefs, mid_other, second_out, mid, part, far_out, near_out, q, second, sems):
    pairs = [
        (own, q.at[:, HALO : HALO + OWN]),
        (near.at[7:11], q.at[:, pl.ds(near_halo(), HALO)]),
        (mid_other, near_out.at[0:4]),
    ]
    run_copies(pairs, sems)
    zero_planes(q, far_beyond(), 1)
    far_out[0:4] = q[:, pl.ds(far_edge(), 1)]
    partial_rates(q, coefs, far_edge(), far_edge() - coef_first(), far_out, 4)
    inner_stages(q, coefs, second, second_out, mid, part)
    near_out[4:8] = mid[...]


def first_kernel(far_at, own, coefs, far_a, far_q, second_in, mid_in, part_in, after, also_after, mid, part, far_out, q, second, third, partial, beyond, raw, sems):
    del after, also_after
    outer, inner = HALO * core(), HALO * (1 - core())
    edge, halo = far_edge(), far_beyond()
    pairs = [
        (own.at[:, pl.ds(outer, HALO)], q.at[:, pl.ds(HALO + outer, HALO)]),
        (far_a.at[0:3], raw),
        (far_q.at[far_at : far_at + 4], q.at[:, pl.ds(halo, 1)]),
        (far_q.at[far_at + 4 : far_at + 8], partial),
        (second_in, second.at[:, pl.ds(3 - 2 * core(), OWN)]),
        (mid_in, mid.at[:, pl.ds(inner, HALO)]),
        (part_in, part.at[:, pl.ds(inner, HALO)]),
    ]
    run_copies(pairs, sems)
    read_beyond(raw, beyond)

    @pl.when(at_end())
    def _():
        zero_planes(q, halo, 1)

    def one(here, rates, plane, row):
        for j in range(4):
            second[j, plane, row : row + TILE, :] = here[j] + (time_step / 2) * rates[j]

    finish_halo(q, partial, coefs, beyond, one)

    @pl.when(at_end())
    def _():
        zero_planes(second, halo, 1)

    over_rates(q, coefs, edge, 1, one, beyond)
    two = second_stage(q, mid, part, HALO)
    over_rates(second, coefs, edge, 1, two, beyond)
    over_rates(second, coefs, edge + 1 - 2 * core(), 1, two)
    third[:, pl.ds(HALO + outer, HALO)] = mid[:, pl.ds(outer, HALO)]
    zero_planes(third, halo, 1)
    far_out[0:4] = third[:, pl.ds(edge, 1)]
    partial_rates(third, coefs, edge, edge - coef_first(), far_out, 4)


def second_kernel(near_at, far_at, own, coefs, near, far_a, far_q, mid, part, far_mid, near_mid, after, out, q, third, fourth, partial, beyond, raw, sems):
    del after
    edge, halo, close = far_edge(), far_beyond(), near_halo()
    mid_at = near_at - 3
    pairs = [
        (own, q.at[:, HALO : HALO + OWN]),
        (near.at[near_at : near_at + 4], q.at[:, pl.ds(close, HALO)]),
        (far_a.at[0:3], raw),
        (far_q.at[far_at : far_at + 4], q.at[:, pl.ds(halo, 1)]),
        (mid, third.at[:, HALO : HALO + OWN]),
        (near_mid.at[mid_at : mid_at + 4], third.at[:, pl.ds(close, HALO)]),
        (far_mid.at[0:4], third.at[:, pl.ds(halo, 1)]),
        (far_mid.at[4:8], partial),
    ]
    run_copies(pairs, sems)
    read_beyond(raw, beyond)

    @pl.when(at_end())
    def _():
        zero_planes(third, halo, 1)

    def one(here, rates, plane, row):
        for j in range(4):
            fourth[j, plane, row : row + TILE, :] = tile_of(q, j, plane, row) + time_step * rates[j]

    finish_halo(third, partial, coefs, beyond, one)

    @pl.when(at_end())
    def _():
        zero_planes(fourth, halo, 1)

    over_rates(third, coefs, edge, 1, one, beyond)
    over_rates(third, coefs, 3 - 2 * core(), OWN, one)

    def two(here, rates, plane, row):
        for j in range(4):
            total = tile_of(part, j, plane - HALO, row) + (1.0 / 3.0) * here[j]
            out[j, plane - HALO, row : row + TILE, :] = total + (time_step / 6) * rates[j]

    over_rates(fourth, coefs, edge, 1, two, beyond)
    over_rates(fourth, coefs, 3 - core(), OWN - 1, two)


def residual_kernel(vec, own, previous, *rest):
    out, held, sems = rest[-3:]
    copies = []
    for j in range(4):
        held[j] = own[j] - previous[j]
        copies.append(pltpu.make_async_copy(held.at[j], out.at[0, vec, j], sems.at[j]))
        copies[-1].start()
    for copy in copies:
        copy.wait()


def shards(state, flow):
    rows, lanes = state.shape[-2:]
    slabs, segs = lax.axis_size("slab"), lax.axis_size("seg")
    near_pairs = [(i, i ^ 1) for i in range(slabs)]
    seg_pairs = [(i, (i + 1) % segs) for i in range(segs)]
    far_pairs = []
    for seg in range(segs):
        for slab in range(slabs):
            if slab in (0, slabs - 1):
                to = (seg ^ 2) * slabs + slab
            else:
                to = seg * slabs + (slab + 1 if slab % 2 else slab - 1)
            far_pairs.append((seg * slabs + slab, to))

    def far_swap(value):
        return lax.ppermute(value, ("seg", "slab"), far_pairs)

    def near_swap(value):
        return lax.ppermute(value, "slab", near_pairs)

    def planes(fields, count):
        return jax.ShapeDtypeStruct((fields, count, rows, lanes), F32)

    def scratch(fields, count):
        return pltpu.VMEM((fields, count, rows, lanes), F32)

    anywhere = pl.BlockSpec(memory_space=pl.ANY)
    vmem = pl.BlockSpec(memory_space=pltpu.VMEM)
    cost = pl.CostEstimate(flops=30_000_000, bytes_accessed=6_000_000, transcendentals=0)
    params = pltpu.CompilerParams(vmem_limit_bytes=16 * 1024 * 1024)

    def call(kernel, name, in_specs, out_shape, scratch_shapes, copies, **options):
        outs = out_shape if isinstance(out_shape, tuple) else (out_shape,)
        return pl.pallas_call(
            kernel,
            out_shape=out_shape,
            in_specs=in_specs,
            out_specs=options.pop("out_specs", (vmem,) * len(outs) if isinstance(out_shape, tuple) else vmem),
            scratch_shapes=scratch_shapes + [pltpu.SemaphoreType.DMA((copies,))],
            compiler_params=params,
            name=name,
            **options,
        )

    state_there = pltpu.with_memory_space_constraint(state, pltpu.HBM)
    flow_there = pltpu.with_memory_space_constraint(flow, pltpu.HBM)
    far_a, near = call(
        pack_kernel,
        "pack",
        [anywhere] * 2,
        (scratch(11, 1), scratch(11, HALO)),
        [scratch(4, 3), scratch(3, 3), scratch(COEFS, 1)],
        7,
    )(state_there, flow_there)
    far_a = far_swap(far_a)
    near = near_swap(near)

    coefs, own0, own1, *inner0 = call(
        inner_0_kernel,
        "inner_0",
        [anywhere] * 3,
        (planes(COEFS, COEF_PLANES), planes(4, OWN), planes(4, OWN), planes(4, OWN), planes(4, HALO), planes(4, HALO)),
        [scratch(4, WIDE), scratch(3, WIDE), scratch(4, WIDE)],
        6,
        cost_estimate=cost,
    )(state_there, flow_there, near)
    *inner1, far_b, near_mid = call(
        inner_1_kernel,
        "inner_1",
        [anywhere, anywhere, vmem, anywhere],
        (planes(4, OWN), planes(4, HALO), planes(4, HALO), planes(8, 1), planes(8, HALO)),
        [scratch(4, WIDE), scratch(4, WIDE)],
        3,
        cost_estimate=cost,
    )(own1, near, coefs, inner0[1])
    far_b = far_swap(far_b)
    near_mid = near_swap(near_mid)

    def first(vec, own, far_at, far_q, ready, *after):
        return call(
            functools.partial(first_kernel, far_at),
            f"first_{vec}",
            [anywhere, vmem] + [anywhere] * 7,
            (planes(4, OWN), planes(4, OWN), planes(8, 1)),
            [scratch(4, WIDE), scratch(4, WIDE), scratch(4, WIDE), scratch(4, 1), scratch(3, 1), scratch(3, 1)],
            7,
            cost_estimate=cost,
        )(own, coefs, far_a, far_q, *ready, *after)

    def second(vec, own, near_at, far_at, far_q, mid, part, far_mid, after):
        return call(
            functools.partial(second_kernel, near_at, far_at),
            f"second_{vec}",
            [anywhere, vmem] + [anywhere] * 4 + [vmem] + [anywhere] * 3,
            planes(4, OWN),
            [scratch(4, WIDE), scratch(4, WIDE), scratch(4, WIDE), scratch(4, 1), scratch(3, 1), scratch(3, 1)],
            8,
            cost_estimate=cost,
        )(own, coefs, near, far_a, far_q, mid, part, far_mid, near_mid, after)

    def residual(vec, own, previous, *buffer):
        return call(
            functools.partial(residual_kernel, vec),
            f"residual_{vec}",
            [vmem, vmem] + [anywhere] * vec,
            pltpu.HBM(state.shape, F32),
            [scratch(4, OWN)],
            4,
            out_specs=anywhere,
            input_output_aliases={2: 0} if vec else {},
        )(own, previous, *buffer)

    mid0, part0, far0 = first(0, own0, 3, far_a, inner0, inner1[1], inner1[1])
    far0 = far_swap(far0)
    mid1, part1, far1 = first(1, own1, 0, far_b, inner1, mid0, mid0)
    far1 = far_swap(far1)
    out0 = second(0, own0, 3, 3, far_a, mid0, part0, far0, mid1)
    prev0 = lax.ppermute(out0, "seg", seg_pairs)
    out1 = second(1, own1, 7, 0, far_b, mid1, part1, far1, out0)
    prev1 = lax.ppermute(out1, "seg", seg_pairs)
    advanced = jnp.stack([out0, out1])[None]
    return advanced, residual(1, own1, prev1, residual(0, own0, prev0))


def solution(mesh):
    return jax.shard_map(
        shards,
        mesh=mesh,
        in_specs=(P("seg", None, None, "slab", None, None), P("seg", None, "slab", None, None)),
        out_specs=(
            P("seg", None, None, "slab", None, None),
            P("seg", None, None, "slab", None, None),
        ),
        check_vma=False,
    )
```

```python
import functools

import jax
import jax.numpy as jnp
from jax import lax
from jax.experimental import pallas as pl
from jax.experimental.pallas import tpu as pltpu
from jax.sharding import PartitionSpec as P

time_step = 0.4
viscosity = 0.067
sound_sq = 1.0

OWN = 4
HALO = 2
WIDE = OWN + 2 * HALO
TILE = 8
COEFS = 12
COEF_PLANES = OWN + 1
F32 = jnp.float32


def core():
    return lax.rem(lax.axis_index("slab"), 2)


def at_end():
    slab = lax.axis_index("slab")
    return jnp.logical_or(slab == 0, slab == lax.axis_size("slab") - 1)


def far_edge():
    return HALO + (OWN - 1) * core()


def far_beyond():
    return HALO - 1 + (OWN + 1) * core()


def near_halo():
    return (1 - core()) * (OWN + HALO)


def coef_first():
    return HALO - core()


def far_sign():
    return 1.0 - 2.0 * core().astype(F32)


def tile_of(ref, field, plane, row):
    return ref[field, plane, row : row + TILE, :]


def around(ref, field, plane, row, rows):
    here = tile_of(ref, field, plane, row)
    index = lax.broadcasted_iota(jnp.int32, here.shape, 0)
    if row == 0:
        y_below = jnp.where(index == 0, 0.0, pltpu.roll(here, 1, 0))
    else:
        y_below = ref[field, plane, row - 1 : row - 1 + TILE, :]
    if row + TILE == rows:
        y_above = jnp.where(index == TILE - 1, 0.0, pltpu.roll(here, TILE - 1, 0))
    else:
        y_above = ref[field, plane, row + 1 : row + 1 + TILE, :]
    lanes = here.shape[1]
    return (
        here,
        tile_of(ref, field, plane - 1, row),
        tile_of(ref, field, plane + 1, row),
        y_below,
        y_above,
        pltpu.roll(here, 1, 1),
        pltpu.roll(here, lanes - 1, 1),
    )


def tile_coefs(base, plane, coefs, place, row, rows):
    for j in range(3):
        b = around(base, j, plane, row, rows)
        coefs[j, place, row : row + TILE, :] = 0.5 * b[0]
        for i in range(3):
            coefs[3 + 3 * i + j, place, row : row + TILE, :] = 0.5 * (b[1 + 2 * i] - b[2 + 2 * i])


def tile_rates(q, coefs, plane, place, row, rows, beyond=None):
    fields = [around(q, j, plane, row, rows) for j in range(4)]
    press = fields[3]
    half = [tile_of(coefs, i, place, row) for i in range(3)]
    lower = [viscosity + h for h in half]
    upper = [viscosity - h for h in half]
    rates = []
    for j in range(3):
        f = fields[j]
        total = (-6.0 * viscosity) * f[0] - 0.5 * (press[2 + 2 * j] - press[1 + 2 * j])
        for i in range(3):
            total = total + lower[i] * f[1 + 2 * i]
            total = total + upper[i] * f[2 + 2 * i]
            total = total + fields[i][0] * tile_of(coefs, 3 + 3 * i + j, place, row)
        if beyond is not None:
            total = total + fields[0][0] * tile_of(beyond, j, 0, row)
        rates.append(total)
    div = (fields[0][2] - fields[0][1]) + (fields[1][4] - fields[1][3])
    div = div + (fields[2][6] - fields[2][5])
    rates.append((-0.5 * sound_sq) * div)
    return [f[0] for f in fields], rates


def over_tiles(first, count, rows, body):
    @pl.loop(first, first + count)
    def _(plane):
        for row in range(0, rows, TILE):
            body(plane, row)


def over_rates(q, coefs, first, count, store, beyond=None):
    rows = q.shape[2]

    def body(plane, row):
        here, rates = tile_rates(q, coefs, plane, plane - coef_first(), row, rows, beyond)
        store(here, rates, plane, row)

    over_tiles(first, count, rows, body)


def partial_rates(q, coefs, plane, place, out, first):
    rows = q.shape[2]
    for row in range(0, rows, TILE):
        _, rates = tile_rates(q, coefs, plane, place, row, rows)
        for j in range(4):
            out[first + j, 0, row : row + TILE, :] = rates[j]


def finish_halo(q, partial, coefs, beyond, store):
    sign, plane, edge = far_sign(), far_beyond(), far_edge()
    place = edge - coef_first()
    for row in range(0, q.shape[2], TILE):
        here = [tile_of(q, j, plane, row) for j in range(4)]
        own = [tile_of(q, j, edge, row) for j in range(4)]
        factor = viscosity - tile_of(beyond, 0, 0, row)
        scaled = sign * here[0]
        rates = [
            tile_of(partial, j, 0, row) + factor * own[j] - scaled * tile_of(coefs, j, place, row)
            for j in range(3)
        ]
        rates[0] = rates[0] - (0.5 * sign) * own[3]
        rates.append(tile_of(partial, 3, 0, row) - (0.5 * sound_sq * sign) * own[0])
        store(here, rates, plane, row)


def start_copies(pairs, sems):
    copies = [pltpu.make_async_copy(a, b, sems.at[i]) for i, (a, b) in enumerate(pairs)]
    for copy in copies:
        copy.start()
    return copies


def run_copies(pairs, sems):
    for copy in start_copies(pairs, sems):
        copy.wait()


def zero_planes(ref, first, width):
    ref[:, pl.ds(first, width)] = jnp.zeros((ref.shape[0], width) + ref.shape[2:], F32)


def read_beyond(flow, ref):
    sign = jnp.where(at_end(), 0.0, 0.5 * far_sign())
    ref[...] = sign * flow[...]


def pack_kernel(state, flow, far_a, near, q, base, coefs, sems):
    far, close = core() * (OWN - HALO), (1 - core()) * (OWN - HALO)
    pairs = [
        (flow.at[0, :, pl.ds(far, HALO)], base.at[:, pl.ds(1 - core(), HALO)]),
        (state.at[0, 0, :, pl.ds(far, HALO)], q.at[:, pl.ds(1 - core(), HALO)]),
        (flow.at[0, :, pl.ds(close, HALO)], near.at[0:3]),
        (state.at[0, 0, :, pl.ds(close, HALO)], near.at[3:7]),
        (state.at[0, 1, :, pl.ds(close, HALO)], near.at[7:11]),
    ]
    copies = start_copies(pairs, sems)
    zero_planes(q, 2 * core(), 1)
    zero_planes(base, 2 * core(), 1)
    copies[0].wait()
    rows = q.shape[2]
    for row in range(0, rows, TILE):
        tile_coefs(base, 1, coefs, 0, row, rows)
    far_a[0:3] = base[:, 1:2]
    copies[1].wait()
    far_a[3:7] = q[:, 1:2]
    partial_rates(q, coefs, 1, 0, far_a, 7)
    for copy in copies[2:]:
        copy.wait()


def inner_stages(q, coefs, second, second_out, mid, part):
    lowest = 3 - 2 * core()

    def one(here, rates, plane, row):
        for j in range(4):
            value = here[j] + (time_step / 2) * rates[j]
            second[j, plane, row : row + TILE, :] = value
            second_out[j, plane - lowest, row : row + TILE, :] = value

    over_rates(q, coefs, lowest, OWN, one)
    over_rates(second, coefs, lowest + 1, HALO, second_stage(q, mid, part, lowest + 1))


def second_stage(q, mid, part, shift):
    def two(here, rates, plane, row):
        for j in range(4):
            start = tile_of(q, j, plane, row)
            third = start + (time_step / 2) * rates[j]
            mid[j, plane - shift, row : row + TILE, :] = third
            part[j, plane - shift, row : row + TILE, :] = (here[j] + 2.0 * third - start) * (1.0 / 3.0)

    return two


def inner_0_kernel(state, flow, near, coefs, own0, own1, second_out, mid, part, q, base, second, sems):
    pairs = [
        (flow.at[0], base.at[:, HALO : HALO + OWN]),
        (near.at[0:3], base.at[:, pl.ds(near_halo(), HALO)]),
        (state.at[0, 0], q.at[:, HALO : HALO + OWN]),
        (near.at[3:7], q.at[:, pl.ds(near_halo(), HALO)]),
        (state.at[0, 0], own0),
        (state.at[0, 1], own1),
    ]
    copies = start_copies(pairs, sems)
    zero_planes(base, far_beyond(), 1)
    for copy in copies[:2]:
        copy.wait()
    rows = q.shape[2]
    over_tiles(
        coef_first(),
        COEF_PLANES,
        rows,
        lambda plane, row: tile_coefs(base, plane, coefs, plane - coef_first(), row, rows),
    )
    for copy in copies[2:]:
        copy.wait()
    inner_stages(q, coefs, second, second_out, mid, part)


def inner_1_kernel(own, near, coefs, mid_other, second_out, mid, part, far_out, near_out, q, second, sems):
    pairs = [
        (own, q.at[:, HALO : HALO + OWN]),
        (near.at[7:11], q.at[:, pl.ds(near_halo(), HALO)]),
        (mid_other, near_out.at[0:4]),
    ]
    run_copies(pairs, sems)
    zero_planes(q, far_beyond(), 1)
    far_out[0:4] = q[:, pl.ds(far_edge(), 1)]
    partial_rates(q, coefs, far_edge(), far_edge() - coef_first(), far_out, 4)
    inner_stages(q, coefs, second, second_out, mid, part)
    near_out[4:8] = mid[...]


def first_kernel(far_at, own, coefs, far_a, far_q, second_in, mid_in, part_in, after, also_after, mid, part, far_out, q, second, third, partial, beyond, raw, sems):
    del after, also_after
    outer, inner = HALO * core(), HALO * (1 - core())
    edge, halo = far_edge(), far_beyond()
    pairs = [
        (own.at[:, pl.ds(outer, HALO)], q.at[:, pl.ds(HALO + outer, HALO)]),
        (far_a.at[0:3], raw),
        (far_q.at[far_at : far_at + 4], q.at[:, pl.ds(halo, 1)]),
        (far_q.at[far_at + 4 : far_at + 8], partial),
        (second_in, second.at[:, pl.ds(3 - 2 * core(), OWN)]),
        (mid_in, mid.at[:, pl.ds(inner, HALO)]),
        (part_in, part.at[:, pl.ds(inner, HALO)]),
    ]
    run_copies(pairs, sems)
    read_beyond(raw, beyond)

    @pl.when(at_end())
    def _():
        zero_planes(q, halo, 1)

    def one(here, rates, plane, row):
        for j in range(4):
            second[j, plane, row : row + TILE, :] = here[j] + (time_step / 2) * rates[j]

    finish_halo(q, partial, coefs, beyond, one)

    @pl.when(at_end())
    def _():
        zero_planes(second, halo, 1)

    over_rates(q, coefs, edge, 1, one, beyond)
    two = second_stage(q, mid, part, HALO)
    over_rates(second, coefs, edge, 1, two, beyond)
    over_rates(second, coefs, edge + 1 - 2 * core(), 1, two)
    third[:, pl.ds(HALO + outer, HALO)] = mid[:, pl.ds(outer, HALO)]
    zero_planes(third, halo, 1)
    far_out[0:4] = third[:, pl.ds(edge, 1)]
    partial_rates(third, coefs, edge, edge - coef_first(), far_out, 4)


def second_kernel(near_at, far_at, own, coefs, near, far_a, far_q, mid, part, far_mid, near_mid, after, out, q, third, fourth, partial, beyond, raw, sems):
    del after
    edge, halo, close = far_edge(), far_beyond(), near_halo()
    mid_at = near_at - 3
    pairs = [
        (own, q.at[:, HALO : HALO + OWN]),
        (near.at[near_at : near_at + 4], q.at[:, pl.ds(close, HALO)]),
        (far_a.at[0:3], raw),
        (far_q.at[far_at : far_at + 4], q.at[:, pl.ds(halo, 1)]),
        (mid, third.at[:, HALO : HALO + OWN]),
        (near_mid.at[mid_at : mid_at + 4], third.at[:, pl.ds(close, HALO)]),
        (far_mid.at[0:4], third.at[:, pl.ds(halo, 1)]),
        (far_mid.at[4:8], partial),
    ]
    run_copies(pairs, sems)
    read_beyond(raw, beyond)

    @pl.when(at_end())
    def _():
        zero_planes(third, halo, 1)

    def one(here, rates, plane, row):
        for j in range(4):
            fourth[j, plane, row : row + TILE, :] = tile_of(q, j, plane, row) + time_step * rates[j]

    finish_halo(third, partial, coefs, beyond, one)

    @pl.when(at_end())
    def _():
        zero_planes(fourth, halo, 1)

    over_rates(third, coefs, edge, 1, one, beyond)
    over_rates(third, coefs, 3 - 2 * core(), OWN, one)

    def two(here, rates, plane, row):
        for j in range(4):
            total = tile_of(part, j, plane - HALO, row) + (1.0 / 3.0) * here[j]
            out[j, plane - HALO, row : row + TILE, :] = total + (time_step / 6) * rates[j]

    over_rates(fourth, coefs, edge, 1, two, beyond)
    over_rates(fourth, coefs, 3 - core(), OWN - 1, two)


def hold_kernel(value, after, out, sems):
    del after
    run_copies([(value, out)], sems)


def residual_kernel(vec, own, previous, *rest):
    out, held, sems = rest[-3:]
    copies = []
    for j in range(4):
        held[j] = own[j] - previous[j]
        copies.append(pltpu.make_async_copy(held.at[j], out.at[0, vec, j], sems.at[j]))
        copies[-1].start()
    for copy in copies:
        copy.wait()


def shards(state, flow):
    rows, lanes = state.shape[-2:]
    slabs, segs = lax.axis_size("slab"), lax.axis_size("seg")
    near_pairs = [(i, i ^ 1) for i in range(slabs)]
    seg_pairs = [(i, (i + 1) % segs) for i in range(segs)]
    far_pairs = []
    for seg in range(segs):
        for slab in range(slabs):
            if slab in (0, slabs - 1):
                to = (seg ^ 2) * slabs + slab
            else:
                to = seg * slabs + (slab + 1 if slab % 2 else slab - 1)
            far_pairs.append((seg * slabs + slab, to))

    def far_swap(value):
        return lax.ppermute(value, ("seg", "slab"), far_pairs)

    def near_swap(value):
        return lax.ppermute(value, "slab", near_pairs)

    def planes(fields, count):
        return jax.ShapeDtypeStruct((fields, count, rows, lanes), F32)

    def scratch(fields, count):
        return pltpu.VMEM((fields, count, rows, lanes), F32)

    anywhere = pl.BlockSpec(memory_space=pl.ANY)
    vmem = pl.BlockSpec(memory_space=pltpu.VMEM)
    cost = pl.CostEstimate(flops=30_000_000, bytes_accessed=6_000_000, transcendentals=0)
    params = pltpu.CompilerParams(vmem_limit_bytes=16 * 1024 * 1024)

    def call(kernel, name, in_specs, out_shape, scratch_shapes, copies, **options):
        outs = out_shape if isinstance(out_shape, tuple) else (out_shape,)
        return pl.pallas_call(
            kernel,
            out_shape=out_shape,
            in_specs=in_specs,
            out_specs=options.pop("out_specs", (vmem,) * len(outs) if isinstance(out_shape, tuple) else vmem),
            scratch_shapes=scratch_shapes + [pltpu.SemaphoreType.DMA((copies,))],
            compiler_params=params,
            name=name,
            **options,
        )

    state_there = pltpu.with_memory_space_constraint(state, pltpu.HBM)
    flow_there = pltpu.with_memory_space_constraint(flow, pltpu.HBM)
    far_a, near = call(
        pack_kernel,
        "pack",
        [anywhere] * 2,
        (scratch(11, 1), scratch(11, HALO)),
        [scratch(4, 3), scratch(3, 3), scratch(COEFS, 1)],
        5,
    )(state_there, flow_there)
    near = near_swap(near)
    far_a = far_swap(far_a)

    coefs, own0, own1, *inner0 = call(
        inner_0_kernel,
        "inner_0",
        [anywhere] * 3,
        (planes(COEFS, COEF_PLANES), planes(4, OWN), planes(4, OWN), planes(4, OWN), planes(4, HALO), planes(4, HALO)),
        [scratch(4, WIDE), scratch(3, WIDE), scratch(4, WIDE)],
        6,
        cost_estimate=cost,
    )(state_there, flow_there, near)
    *inner1, far_b, near_mid = call(
        inner_1_kernel,
        "inner_1",
        [anywhere, anywhere, vmem, anywhere],
        (planes(4, OWN), planes(4, HALO), planes(4, HALO), planes(8, 1), planes(8, HALO)),
        [scratch(4, WIDE), scratch(4, WIDE)],
        3,
        cost_estimate=cost,
    )(own1, near, coefs, inner0[1])
    far_b = far_swap(far_b)
    near_mid = near_swap(near_mid)

    def first(vec, own, far_at, far_q, ready, *after):
        return call(
            functools.partial(first_kernel, far_at),
            f"first_{vec}",
            [anywhere, vmem] + [anywhere] * 7,
            (planes(4, OWN), planes(4, OWN), planes(8, 1)),
            [scratch(4, WIDE), scratch(4, WIDE), scratch(4, WIDE), scratch(4, 1), scratch(3, 1), scratch(3, 1)],
            7,
            cost_estimate=cost,
        )(own, coefs, far_a, far_q, *ready, *after)

    def second(vec, own, near_at, far_at, far_q, mid, part, far_mid, after):
        return call(
            functools.partial(second_kernel, near_at, far_at),
            f"second_{vec}",
            [anywhere, vmem] + [anywhere] * 4 + [vmem] + [anywhere] * 3,
            planes(4, OWN),
            [scratch(4, WIDE), scratch(4, WIDE), scratch(4, WIDE), scratch(4, 1), scratch(3, 1), scratch(3, 1)],
            8,
            cost_estimate=cost,
        )(own, coefs, near, far_a, far_q, mid, part, far_mid, near_mid, after)

    def residual(vec, own, previous, *buffer):
        return call(
            functools.partial(residual_kernel, vec),
            f"residual_{vec}",
            [vmem, vmem] + [anywhere] * vec,
            pltpu.HBM(state.shape, F32),
            [scratch(4, OWN)],
            4,
            out_specs=anywhere,
            input_output_aliases={2: 0} if vec else {},
        )(own, previous, *buffer)

    mid0, part0, far0 = first(0, own0, 3, far_a, inner0, inner1[1], inner1[1])
    far0 = far_swap(far0)
    mid1, part1, far1 = first(1, own1, 0, far_b, inner1, mid0, mid0)
    far1 = far_swap(far1)
    out0 = second(0, own0, 3, 3, far_a, mid0, part0, far0, mid1)
    held0 = call(hold_kernel, "hold", [anywhere] * 2, scratch(4, OWN), [], 1)(out0, far1)
    prev0 = lax.ppermute(held0, "seg", seg_pairs)
    out1 = second(1, own1, 7, 0, far_b, mid1, part1, far1, out0)
    prev1 = lax.ppermute(out1, "seg", seg_pairs)
    advanced = jnp.stack([out0, out1])[None]
    return advanced, residual(1, own1, prev1, residual(0, own0, prev0))


def solution(mesh):
    return jax.shard_map(
        shards,
        mesh=mesh,
        in_specs=(P("seg", None, None, "slab", None, None), P("seg", None, "slab", None, None)),
        out_specs=(
            P("seg", None, None, "slab", None, None),
            P("seg", None, None, "slab", None, None),
        ),
        check_vma=False,
    )
```

```python
import functools

import jax
import jax.numpy as jnp
from jax import lax
from jax.experimental import pallas as pl
from jax.experimental.pallas import tpu as pltpu
from jax.sharding import PartitionSpec as P

time_step = 0.4
viscosity = 0.067
sound_sq = 1.0

OWN = 4
HALO = 2
WIDE = OWN + 2 * HALO
TILE = 8
COEFS = 12
COEF_PLANES = OWN + 1
F32 = jnp.float32


def core():
    return lax.rem(lax.axis_index("slab"), 2)


def at_end():
    slab = lax.axis_index("slab")
    return jnp.logical_or(slab == 0, slab == lax.axis_size("slab") - 1)


def far_edge():
    return HALO + (OWN - 1) * core()


def far_beyond():
    return HALO - 1 + (OWN + 1) * core()


def near_halo():
    return (1 - core()) * (OWN + HALO)


def coef_first():
    return HALO - core()


def far_sign():
    return 1.0 - 2.0 * core().astype(F32)


def tile_of(ref, field, plane, row):
    return ref[field, plane, row : row + TILE, :]


def around(ref, field, plane, row, rows):
    here = tile_of(ref, field, plane, row)
    index = lax.broadcasted_iota(jnp.int32, here.shape, 0)
    if row == 0:
        y_below = jnp.where(index == 0, 0.0, pltpu.roll(here, 1, 0))
    else:
        y_below = ref[field, plane, row - 1 : row - 1 + TILE, :]
    if row + TILE == rows:
        y_above = jnp.where(index == TILE - 1, 0.0, pltpu.roll(here, TILE - 1, 0))
    else:
        y_above = ref[field, plane, row + 1 : row + 1 + TILE, :]
    lanes = here.shape[1]
    return (
        here,
        tile_of(ref, field, plane - 1, row),
        tile_of(ref, field, plane + 1, row),
        y_below,
        y_above,
        pltpu.roll(here, 1, 1),
        pltpu.roll(here, lanes - 1, 1),
    )


def tile_coefs(base, plane, coefs, place, row, rows):
    for j in range(3):
        b = around(base, j, plane, row, rows)
        coefs[j, place, row : row + TILE, :] = 0.5 * b[0]
        for i in range(3):
            coefs[3 + 3 * i + j, place, row : row + TILE, :] = 0.5 * (b[1 + 2 * i] - b[2 + 2 * i])


def tile_rates(q, coefs, plane, place, row, rows, beyond=None):
    fields = [around(q, j, plane, row, rows) for j in range(4)]
    press = fields[3]
    half = [tile_of(coefs, i, place, row) for i in range(3)]
    lower = [viscosity + h for h in half]
    upper = [viscosity - h for h in half]
    rates = []
    for j in range(3):
        f = fields[j]
        total = (-6.0 * viscosity) * f[0] - 0.5 * (press[2 + 2 * j] - press[1 + 2 * j])
        for i in range(3):
            total = total + lower[i] * f[1 + 2 * i]
            total = total + upper[i] * f[2 + 2 * i]
            total = total + fields[i][0] * tile_of(coefs, 3 + 3 * i + j, place, row)
        if beyond is not None:
            total = total + fields[0][0] * tile_of(beyond, j, 0, row)
        rates.append(total)
    div = (fields[0][2] - fields[0][1]) + (fields[1][4] - fields[1][3])
    div = div + (fields[2][6] - fields[2][5])
    rates.append((-0.5 * sound_sq) * div)
    return [f[0] for f in fields], rates


def over_tiles(first, count, rows, body):
    @pl.loop(first, first + count)
    def _(plane):
        for row in range(0, rows, TILE):
            body(plane, row)


def over_rates(q, coefs, first, count, store, beyond=None):
    rows = q.shape[2]

    def body(plane, row):
        here, rates = tile_rates(q, coefs, plane, plane - coef_first(), row, rows, beyond)
        store(here, rates, plane, row)

    over_tiles(first, count, rows, body)


def partial_rates(q, coefs, plane, place, out, first):
    rows = q.shape[2]
    for row in range(0, rows, TILE):
        _, rates = tile_rates(q, coefs, plane, place, row, rows)
        for j in range(4):
            out[first + j, 0, row : row + TILE, :] = rates[j]


def finish_halo(q, partial, coefs, beyond, store):
    sign, plane, edge = far_sign(), far_beyond(), far_edge()
    place = edge - coef_first()
    for row in range(0, q.shape[2], TILE):
        here = [tile_of(q, j, plane, row) for j in range(4)]
        own = [tile_of(q, j, edge, row) for j in range(4)]
        factor = viscosity - tile_of(beyond, 0, 0, row)
        scaled = sign * here[0]
        rates = [
            tile_of(partial, j, 0, row) + factor * own[j] - scaled * tile_of(coefs, j, place, row)
            for j in range(3)
        ]
        rates[0] = rates[0] - (0.5 * sign) * own[3]
        rates.append(tile_of(partial, 3, 0, row) - (0.5 * sound_sq * sign) * own[0])
        store(here, rates, plane, row)


def start_copies(pairs, sems):
    copies = [pltpu.make_async_copy(a, b, sems.at[i]) for i, (a, b) in enumerate(pairs)]
    for copy in copies:
        copy.start()
    return copies


def run_copies(pairs, sems):
    for copy in start_copies(pairs, sems):
        copy.wait()


def zero_planes(ref, first, width):
    ref[:, pl.ds(first, width)] = jnp.zeros((ref.shape[0], width) + ref.shape[2:], F32)


def read_beyond(flow, ref):
    sign = jnp.where(at_end(), 0.0, 0.5 * far_sign())
    ref[...] = sign * flow[...]


def pack_kernel(state, flow, far_a, near, q, base, coefs, sems):
    close, edge = (1 - core()) * (OWN - HALO), 1 + core() * (OWN - 1)
    pairs = [
        (flow.at[0], base.at[:, 1 : 1 + OWN]),
        (state.at[0, 0], q.at[:, 1 : 1 + OWN]),
        (state.at[0, 1, :, pl.ds(close, HALO)], near.at[7:11]),
    ]
    copies = start_copies(pairs, sems)
    zero_planes(q, core() * (OWN + 1), 1)
    zero_planes(base, core() * (OWN + 1), 1)
    copies[0].wait()
    rows = q.shape[2]
    for row in range(0, rows, TILE):
        tile_coefs(base, edge, coefs, 0, row, rows)
    far_a[0:3] = base[:, pl.ds(edge, 1)]
    near[0:3] = base[:, pl.ds(1 + close, HALO)]
    copies[1].wait()
    far_a[3:7] = q[:, pl.ds(edge, 1)]
    near[3:7] = q[:, pl.ds(1 + close, HALO)]
    partial_rates(q, coefs, edge, 0, far_a, 7)
    copies[2].wait()


def inner_stages(q, coefs, second, second_out, mid, part):
    lowest = 3 - 2 * core()

    def one(here, rates, plane, row):
        for j in range(4):
            value = here[j] + (time_step / 2) * rates[j]
            second[j, plane, row : row + TILE, :] = value
            second_out[j, plane - lowest, row : row + TILE, :] = value

    over_rates(q, coefs, lowest, OWN, one)
    over_rates(second, coefs, lowest + 1, HALO, second_stage(q, mid, part, lowest + 1))


def second_stage(q, mid, part, shift):
    def two(here, rates, plane, row):
        for j in range(4):
            start = tile_of(q, j, plane, row)
            third = start + (time_step / 2) * rates[j]
            mid[j, plane - shift, row : row + TILE, :] = third
            part[j, plane - shift, row : row + TILE, :] = (here[j] + 2.0 * third - start) * (1.0 / 3.0)

    return two


def inner_0_kernel(state, flow, near, coefs, own0, own1, second_out, mid, part, q, base, second, sems):
    pairs = [
        (flow.at[0], base.at[:, HALO : HALO + OWN]),
        (near.at[0:3], base.at[:, pl.ds(near_halo(), HALO)]),
        (state.at[0, 0], q.at[:, HALO : HALO + OWN]),
        (near.at[3:7], q.at[:, pl.ds(near_halo(), HALO)]),
        (state.at[0, 0], own0),
        (state.at[0, 1], own1),
    ]
    copies = start_copies(pairs, sems)
    zero_planes(base, far_beyond(), 1)
    for copy in copies[:2]:
        copy.wait()
    rows = q.shape[2]
    over_tiles(
        coef_first(),
        COEF_PLANES,
        rows,
        lambda plane, row: tile_coefs(base, plane, coefs, plane - coef_first(), row, rows),
    )
    for copy in copies[2:]:
        copy.wait()
    inner_stages(q, coefs, second, second_out, mid, part)


def inner_1_kernel(own, near, coefs, mid_other, second_out, mid, part, far_out, near_out, q, second, sems):
    pairs = [
        (own, q.at[:, HALO : HALO + OWN]),
        (near.at[7:11], q.at[:, pl.ds(near_halo(), HALO)]),
        (mid_other, near_out.at[0:4]),
    ]
    run_copies(pairs, sems)
    zero_planes(q, far_beyond(), 1)
    far_out[0:4] = q[:, pl.ds(far_edge(), 1)]
    partial_rates(q, coefs, far_edge(), far_edge() - coef_first(), far_out, 4)
    inner_stages(q, coefs, second, second_out, mid, part)
    near_out[4:8] = mid[...]


def first_kernel(far_at, own, coefs, far_a, far_q, second_in, mid_in, part_in, after, also_after, mid, part, far_out, q, second, third, partial, beyond, raw, sems):
    del after, also_after
    outer, inner = HALO * core(), HALO * (1 - core())
    edge, halo = far_edge(), far_beyond()
    pairs = [
        (own.at[:, pl.ds(outer, HALO)], q.at[:, pl.ds(HALO + outer, HALO)]),
        (far_a.at[0:3], raw),
        (far_q.at[far_at : far_at + 4], q.at[:, pl.ds(halo, 1)]),
        (far_q.at[far_at + 4 : far_at + 8], partial),
        (second_in, second.at[:, pl.ds(3 - 2 * core(), OWN)]),
        (mid_in, mid.at[:, pl.ds(inner, HALO)]),
        (part_in, part.at[:, pl.ds(inner, HALO)]),
    ]
    run_copies(pairs, sems)
    read_beyond(raw, beyond)

    @pl.when(at_end())
    def _():
        zero_planes(q, halo, 1)

    def one(here, rates, plane, row):
        for j in range(4):
            second[j, plane, row : row + TILE, :] = here[j] + (time_step / 2) * rates[j]

    finish_halo(q, partial, coefs, beyond, one)

    @pl.when(at_end())
    def _():
        zero_planes(second, halo, 1)

    over_rates(q, coefs, edge, 1, one, beyond)
    two = second_stage(q, mid, part, HALO)
    over_rates(second, coefs, edge, 1, two, beyond)
    over_rates(second, coefs, edge + 1 - 2 * core(), 1, two)
    third[:, pl.ds(HALO + outer, HALO)] = mid[:, pl.ds(outer, HALO)]
    zero_planes(third, halo, 1)
    far_out[0:4] = third[:, pl.ds(edge, 1)]
    partial_rates(third, coefs, edge, edge - coef_first(), far_out, 4)


def second_kernel(near_at, far_at, own, coefs, near, far_a, far_q, mid, part, far_mid, near_mid, after, out, q, third, fourth, partial, beyond, raw, sems):
    del after
    edge, halo, close = far_edge(), far_beyond(), near_halo()
    mid_at = near_at - 3
    pairs = [
        (own, q.at[:, HALO : HALO + OWN]),
        (near.at[near_at : near_at + 4], q.at[:, pl.ds(close, HALO)]),
        (far_a.at[0:3], raw),
        (far_q.at[far_at : far_at + 4], q.at[:, pl.ds(halo, 1)]),
        (mid, third.at[:, HALO : HALO + OWN]),
        (near_mid.at[mid_at : mid_at + 4], third.at[:, pl.ds(close, HALO)]),
        (far_mid.at[0:4], third.at[:, pl.ds(halo, 1)]),
        (far_mid.at[4:8], partial),
    ]
    run_copies(pairs, sems)
    read_beyond(raw, beyond)

    @pl.when(at_end())
    def _():
        zero_planes(third, halo, 1)

    def one(here, rates, plane, row):
        for j in range(4):
            fourth[j, plane, row : row + TILE, :] = tile_of(q, j, plane, row) + time_step * rates[j]

    finish_halo(third, partial, coefs, beyond, one)

    @pl.when(at_end())
    def _():
        zero_planes(fourth, halo, 1)

    over_rates(third, coefs, edge, 1, one, beyond)
    over_rates(third, coefs, 3 - 2 * core(), OWN, one)

    def two(here, rates, plane, row):
        for j in range(4):
            total = tile_of(part, j, plane - HALO, row) + (1.0 / 3.0) * here[j]
            out[j, plane - HALO, row : row + TILE, :] = total + (time_step / 6) * rates[j]

    over_rates(fourth, coefs, edge, 1, two, beyond)
    over_rates(fourth, coefs, 3 - core(), OWN - 1, two)


def hold_kernel(value, after, out, sems):
    del after
    run_copies([(value, out)], sems)


def residual_kernel(vec, own, previous, *rest):
    out, held, sems = rest[-3:]
    copies = []
    for j in range(4):
        held[j] = own[j] - previous[j]
        copies.append(pltpu.make_async_copy(held.at[j], out.at[0, vec, j], sems.at[j]))
        copies[-1].start()
    for copy in copies:
        copy.wait()


def shards(state, flow):
    rows, lanes = state.shape[-2:]
    slabs, segs = lax.axis_size("slab"), lax.axis_size("seg")
    near_pairs = [(i, i ^ 1) for i in range(slabs)]
    seg_pairs = [(i, (i + 1) % segs) for i in range(segs)]
    far_pairs = []
    for seg in range(segs):
        for slab in range(slabs):
            if slab in (0, slabs - 1):
                to = (seg ^ 2) * slabs + slab
            else:
                to = seg * slabs + (slab + 1 if slab % 2 else slab - 1)
            far_pairs.append((seg * slabs + slab, to))

    def far_swap(value):
        return lax.ppermute(value, ("seg", "slab"), far_pairs)

    def near_swap(value):
        return lax.ppermute(value, "slab", near_pairs)

    def planes(fields, count):
        return jax.ShapeDtypeStruct((fields, count, rows, lanes), F32)

    def scratch(fields, count):
        return pltpu.VMEM((fields, count, rows, lanes), F32)

    anywhere = pl.BlockSpec(memory_space=pl.ANY)
    vmem = pl.BlockSpec(memory_space=pltpu.VMEM)
    cost = pl.CostEstimate(flops=30_000_000, bytes_accessed=6_000_000, transcendentals=0)
    params = pltpu.CompilerParams(vmem_limit_bytes=16 * 1024 * 1024)

    def call(kernel, name, in_specs, out_shape, scratch_shapes, copies, **options):
        outs = out_shape if isinstance(out_shape, tuple) else (out_shape,)
        return pl.pallas_call(
            kernel,
            out_shape=out_shape,
            in_specs=in_specs,
            out_specs=options.pop("out_specs", (vmem,) * len(outs) if isinstance(out_shape, tuple) else vmem),
            scratch_shapes=scratch_shapes + [pltpu.SemaphoreType.DMA((copies,))],
            compiler_params=params,
            name=name,
            **options,
        )

    state_there = pltpu.with_memory_space_constraint(state, pltpu.HBM)
    flow_there = pltpu.with_memory_space_constraint(flow, pltpu.HBM)
    far_a, near = call(
        pack_kernel,
        "pack",
        [anywhere] * 2,
        (scratch(11, 1), scratch(11, HALO)),
        [scratch(4, OWN + 2), scratch(3, OWN + 2), scratch(COEFS, 1)],
        3,
    )(state_there, flow_there)
    near = near_swap(near)
    far_a = far_swap(far_a)

    coefs, own0, own1, *inner0 = call(
        inner_0_kernel,
        "inner_0",
        [anywhere] * 3,
        (planes(COEFS, COEF_PLANES), planes(4, OWN), planes(4, OWN), planes(4, OWN), planes(4, HALO), planes(4, HALO)),
        [scratch(4, WIDE), scratch(3, WIDE), scratch(4, WIDE)],
        6,
        cost_estimate=cost,
    )(state_there, flow_there, near)
    *inner1, far_b, near_mid = call(
        inner_1_kernel,
        "inner_1",
        [anywhere, anywhere, vmem, anywhere],
        (planes(4, OWN), planes(4, HALO), planes(4, HALO), planes(8, 1), planes(8, HALO)),
        [scratch(4, WIDE), scratch(4, WIDE)],
        3,
        cost_estimate=cost,
    )(own1, near, coefs, inner0[1])
    far_b = far_swap(far_b)
    near_mid = near_swap(near_mid)

    def first(vec, own, far_at, far_q, ready, *after):
        return call(
            functools.partial(first_kernel, far_at),
            f"first_{vec}",
            [anywhere, vmem] + [anywhere] * 7,
            (planes(4, OWN), planes(4, OWN), planes(8, 1)),
            [scratch(4, WIDE), scratch(4, WIDE), scratch(4, WIDE), scratch(4, 1), scratch(3, 1), scratch(3, 1)],
            7,
            cost_estimate=cost,
        )(own, coefs, far_a, far_q, *ready, *after)

    def second(vec, own, near_at, far_at, far_q, mid, part, far_mid, after):
        return call(
            functools.partial(second_kernel, near_at, far_at),
            f"second_{vec}",
            [anywhere, vmem] + [anywhere] * 4 + [vmem] + [anywhere] * 3,
            planes(4, OWN),
            [scratch(4, WIDE), scratch(4, WIDE), scratch(4, WIDE), scratch(4, 1), scratch(3, 1), scratch(3, 1)],
            8,
            cost_estimate=cost,
        )(own, coefs, near, far_a, far_q, mid, part, far_mid, near_mid, after)

    def residual(vec, own, previous, *buffer):
        return call(
            functools.partial(residual_kernel, vec),
            f"residual_{vec}",
            [vmem, vmem] + [anywhere] * vec,
            pltpu.HBM(state.shape, F32),
            [scratch(4, OWN)],
            4,
            out_specs=anywhere,
            input_output_aliases={2: 0} if vec else {},
        )(own, previous, *buffer)

    mid0, part0, far0 = first(0, own0, 3, far_a, inner0, inner1[1], inner1[1])
    far0 = far_swap(far0)
    mid1, part1, far1 = first(1, own1, 0, far_b, inner1, mid0, mid0)
    far1 = far_swap(far1)
    out0 = second(0, own0, 3, 3, far_a, mid0, part0, far0, mid1)
    held0 = call(hold_kernel, "hold", [anywhere] * 2, scratch(4, OWN), [], 1)(out0, far1)
    prev0 = lax.ppermute(held0, "seg", seg_pairs)
    out1 = second(1, own1, 7, 0, far_b, mid1, part1, far1, out0)
    prev1 = lax.ppermute(out1, "seg", seg_pairs)
    advanced = jnp.stack([out0, out1])[None]
    return advanced, residual(1, own1, prev1, residual(0, own0, prev0))


def solution(mesh):
    return jax.shard_map(
        shards,
        mesh=mesh,
        in_specs=(P("seg", None, None, "slab", None, None), P("seg", None, "slab", None, None)),
        out_specs=(
            P("seg", None, None, "slab", None, None),
            P("seg", None, None, "slab", None, None),
        ),
        check_vma=False,
    )
```

```python
import functools

import jax
import jax.numpy as jnp
from jax import lax
from jax.experimental import pallas as pl
from jax.experimental.pallas import tpu as pltpu
from jax.sharding import PartitionSpec as P

time_step = 0.4
viscosity = 0.067
sound_sq = 1.0

OWN = 4
HALO = 2
WIDE = OWN + 2 * HALO
TILE = 8
COEFS = 12
COEF_PLANES = OWN + 1
F32 = jnp.float32


def core():
    return lax.rem(lax.axis_index("slab"), 2)


def at_end():
    slab = lax.axis_index("slab")
    return jnp.logical_or(slab == 0, slab == lax.axis_size("slab") - 1)


def far_edge():
    return HALO + (OWN - 1) * core()


def far_beyond():
    return HALO - 1 + (OWN + 1) * core()


def near_halo():
    return (1 - core()) * (OWN + HALO)


def coef_first():
    return HALO - core()


def far_sign():
    return 1.0 - 2.0 * core().astype(F32)


def tile_of(ref, field, plane, row):
    return ref[field, plane, row : row + TILE, :]


def around(ref, field, plane, row, rows):
    here = tile_of(ref, field, plane, row)
    index = lax.broadcasted_iota(jnp.int32, here.shape, 0)
    if row == 0:
        y_below = jnp.where(index == 0, 0.0, pltpu.roll(here, 1, 0))
    else:
        y_below = ref[field, plane, row - 1 : row - 1 + TILE, :]
    if row + TILE == rows:
        y_above = jnp.where(index == TILE - 1, 0.0, pltpu.roll(here, TILE - 1, 0))
    else:
        y_above = ref[field, plane, row + 1 : row + 1 + TILE, :]
    lanes = here.shape[1]
    return (
        here,
        tile_of(ref, field, plane - 1, row),
        tile_of(ref, field, plane + 1, row),
        y_below,
        y_above,
        pltpu.roll(here, 1, 1),
        pltpu.roll(here, lanes - 1, 1),
    )


def tile_coefs(base, plane, coefs, place, row, rows):
    for j in range(3):
        b = around(base, j, plane, row, rows)
        coefs[j, place, row : row + TILE, :] = 0.5 * b[0]
        for i in range(3):
            coefs[3 + 3 * i + j, place, row : row + TILE, :] = 0.5 * (b[1 + 2 * i] - b[2 + 2 * i])


def tile_rates(q, coefs, plane, place, row, rows, beyond=None):
    fields = [around(q, j, plane, row, rows) for j in range(4)]
    press = fields[3]
    half = [tile_of(coefs, i, place, row) for i in range(3)]
    lower = [viscosity + h for h in half]
    upper = [viscosity - h for h in half]
    rates = []
    for j in range(3):
        f = fields[j]
        total = (-6.0 * viscosity) * f[0] - 0.5 * (press[2 + 2 * j] - press[1 + 2 * j])
        for i in range(3):
            total = total + lower[i] * f[1 + 2 * i]
            total = total + upper[i] * f[2 + 2 * i]
            total = total + fields[i][0] * tile_of(coefs, 3 + 3 * i + j, place, row)
        if beyond is not None:
            total = total + fields[0][0] * tile_of(beyond, j, 0, row)
        rates.append(total)
    div = (fields[0][2] - fields[0][1]) + (fields[1][4] - fields[1][3])
    div = div + (fields[2][6] - fields[2][5])
    rates.append((-0.5 * sound_sq) * div)
    return [f[0] for f in fields], rates


def over_tiles(first, count, rows, body):
    @pl.loop(first, first + count)
    def _(plane):
        for row in range(0, rows, TILE):
            body(plane, row)


def over_rates(q, coefs, first, count, store, beyond=None):
    rows = q.shape[2]

    def body(plane, row):
        here, rates = tile_rates(q, coefs, plane, plane - coef_first(), row, rows, beyond)
        store(here, rates, plane, row)

    over_tiles(first, count, rows, body)


def partial_rates(q, coefs, plane, place, out, first):
    rows = q.shape[2]
    for row in range(0, rows, TILE):
        _, rates = tile_rates(q, coefs, plane, place, row, rows)
        for j in range(4):
            out[first + j, 0, row : row + TILE, :] = rates[j]


def finish_halo(q, partial, coefs, beyond, store):
    sign, plane, edge = far_sign(), far_beyond(), far_edge()
    place = edge - coef_first()
    for row in range(0, q.shape[2], TILE):
        here = [tile_of(q, j, plane, row) for j in range(4)]
        own = [tile_of(q, j, edge, row) for j in range(4)]
        factor = viscosity - tile_of(beyond, 0, 0, row)
        scaled = sign * here[0]
        rates = [
            tile_of(partial, j, 0, row) + factor * own[j] - scaled * tile_of(coefs, j, place, row)
            for j in range(3)
        ]
        rates[0] = rates[0] - (0.5 * sign) * own[3]
        rates.append(tile_of(partial, 3, 0, row) - (0.5 * sound_sq * sign) * own[0])
        store(here, rates, plane, row)


def start_copies(pairs, sems):
    copies = [pltpu.make_async_copy(a, b, sems.at[i]) for i, (a, b) in enumerate(pairs)]
    for copy in copies:
        copy.start()
    return copies


def run_copies(pairs, sems):
    for copy in start_copies(pairs, sems):
        copy.wait()


def zero_planes(ref, first, width):
    ref[:, pl.ds(first, width)] = jnp.zeros((ref.shape[0], width) + ref.shape[2:], F32)


def read_beyond(flow, ref):
    sign = jnp.where(at_end(), 0.0, 0.5 * far_sign())
    ref[...] = sign * flow[...]


def pack_kernel(state, flow, far_a, near, q, base, coefs, sems):
    far, close = core() * (OWN - HALO), (1 - core()) * (OWN - HALO)
    pairs = [
        (flow.at[0, :, pl.ds(far, HALO)], base.at[:, pl.ds(1 - core(), HALO)]),
        (state.at[0, 0, :, pl.ds(far, HALO)], q.at[:, pl.ds(1 - core(), HALO)]),
        (flow.at[0, :, pl.ds(close, HALO)], near.at[0:3]),
        (state.at[0, 0, :, pl.ds(close, HALO)], near.at[3:7]),
        (state.at[0, 1, :, pl.ds(close, HALO)], near.at[7:11]),
    ]
    copies = start_copies(pairs, sems)
    zero_planes(q, 2 * core(), 1)
    zero_planes(base, 2 * core(), 1)
    copies[0].wait()
    rows = q.shape[2]
    for row in range(0, rows, TILE):
        tile_coefs(base, 1, coefs, 0, row, rows)
    far_a[0:3] = base[:, 1:2]
    copies[1].wait()
    far_a[3:7] = q[:, 1:2]
    partial_rates(q, coefs, 1, 0, far_a, 7)
    for copy in copies[2:]:
        copy.wait()


def inner_stages(q, coefs, second, second_out, mid, part):
    lowest = 3 - 2 * core()

    def one(here, rates, plane, row):
        for j in range(4):
            value = here[j] + (time_step / 2) * rates[j]
            second[j, plane, row : row + TILE, :] = value
            second_out[j, plane - lowest, row : row + TILE, :] = value

    over_rates(q, coefs, lowest, OWN, one)
    over_rates(second, coefs, lowest + 1, HALO, second_stage(q, mid, part, lowest + 1))


def second_stage(q, mid, part, shift):
    def two(here, rates, plane, row):
        for j in range(4):
            start = tile_of(q, j, plane, row)
            third = start + (time_step / 2) * rates[j]
            mid[j, plane - shift, row : row + TILE, :] = third
            part[j, plane - shift, row : row + TILE, :] = (here[j] + 2.0 * third - start) * (1.0 / 3.0)

    return two


def inner_0_kernel(state, flow, near, coefs, own0, own1, second_out, mid, part, q, base, second, sems):
    pairs = [
        (flow.at[0], base.at[:, HALO : HALO + OWN]),
        (near.at[0:3], base.at[:, pl.ds(near_halo(), HALO)]),
        (state.at[0, 0], q.at[:, HALO : HALO + OWN]),
        (near.at[3:7], q.at[:, pl.ds(near_halo(), HALO)]),
        (state.at[0, 0], own0),
        (state.at[0, 1], own1),
    ]
    copies = start_copies(pairs, sems)
    zero_planes(base, far_beyond(), 1)
    for copy in copies[:2]:
        copy.wait()
    rows = q.shape[2]
    over_tiles(
        coef_first(),
        COEF_PLANES,
        rows,
        lambda plane, row: tile_coefs(base, plane, coefs, plane - coef_first(), row, rows),
    )
    for copy in copies[2:]:
        copy.wait()
    inner_stages(q, coefs, second, second_out, mid, part)


def inner_1_kernel(own, near, coefs, mid_other, second_out, mid, part, far_out, near_out, q, second, sems):
    pairs = [
        (own, q.at[:, HALO : HALO + OWN]),
        (near.at[7:11], q.at[:, pl.ds(near_halo(), HALO)]),
        (mid_other, near_out.at[0:4]),
    ]
    run_copies(pairs, sems)
    zero_planes(q, far_beyond(), 1)
    far_out[0:4] = q[:, pl.ds(far_edge(), 1)]
    partial_rates(q, coefs, far_edge(), far_edge() - coef_first(), far_out, 4)
    inner_stages(q, coefs, second, second_out, mid, part)
    near_out[4:8] = mid[...]


def first_kernel(far_at, own, coefs, far_a, far_q, second_in, mid_in, part_in, after, also_after, mid, part, far_out, q, second, third, partial, beyond, raw, sems):
    del after, also_after
    outer, inner = HALO * core(), HALO * (1 - core())
    edge, halo = far_edge(), far_beyond()
    pairs = [
        (own.at[:, pl.ds(outer, HALO)], q.at[:, pl.ds(HALO + outer, HALO)]),
        (far_a.at[0:3], raw),
        (far_q.at[far_at : far_at + 4], q.at[:, pl.ds(halo, 1)]),
        (far_q.at[far_at + 4 : far_at + 8], partial),
        (second_in, second.at[:, pl.ds(3 - 2 * core(), OWN)]),
        (mid_in, mid.at[:, pl.ds(inner, HALO)]),
        (part_in, part.at[:, pl.ds(inner, HALO)]),
    ]
    run_copies(pairs, sems)
    read_beyond(raw, beyond)

    @pl.when(at_end())
    def _():
        zero_planes(q, halo, 1)

    def one(here, rates, plane, row):
        for j in range(4):
            second[j, plane, row : row + TILE, :] = here[j] + (time_step / 2) * rates[j]

    finish_halo(q, partial, coefs, beyond, one)

    @pl.when(at_end())
    def _():
        zero_planes(second, halo, 1)

    over_rates(q, coefs, edge, 1, one, beyond)
    two = second_stage(q, mid, part, HALO)
    over_rates(second, coefs, edge, 1, two, beyond)
    over_rates(second, coefs, edge + 1 - 2 * core(), 1, two)
    third[:, pl.ds(HALO + outer, HALO)] = mid[:, pl.ds(outer, HALO)]
    zero_planes(third, halo, 1)
    far_out[0:4] = third[:, pl.ds(edge, 1)]
    partial_rates(third, coefs, edge, edge - coef_first(), far_out, 4)


def second_kernel(near_at, far_at, own, coefs, near, far_a, far_q, mid, part, far_mid, near_mid, after, out, q, third, fourth, partial, beyond, raw, sems):
    del after
    edge, halo, close = far_edge(), far_beyond(), near_halo()
    mid_at = near_at - 3
    pairs = [
        (own, q.at[:, HALO : HALO + OWN]),
        (near.at[near_at : near_at + 4], q.at[:, pl.ds(close, HALO)]),
        (far_a.at[0:3], raw),
        (far_q.at[far_at : far_at + 4], q.at[:, pl.ds(halo, 1)]),
        (mid, third.at[:, HALO : HALO + OWN]),
        (near_mid.at[mid_at : mid_at + 4], third.at[:, pl.ds(close, HALO)]),
        (far_mid.at[0:4], third.at[:, pl.ds(halo, 1)]),
        (far_mid.at[4:8], partial),
    ]
    run_copies(pairs, sems)
    read_beyond(raw, beyond)

    @pl.when(at_end())
    def _():
        zero_planes(third, halo, 1)

    def one(here, rates, plane, row):
        for j in range(4):
            fourth[j, plane, row : row + TILE, :] = tile_of(q, j, plane, row) + time_step * rates[j]

    finish_halo(third, partial, coefs, beyond, one)

    @pl.when(at_end())
    def _():
        zero_planes(fourth, halo, 1)

    over_rates(third, coefs, edge, 1, one, beyond)
    over_rates(third, coefs, 3 - 2 * core(), OWN, one)

    def two(here, rates, plane, row):
        for j in range(4):
            total = tile_of(part, j, plane - HALO, row) + (1.0 / 3.0) * here[j]
            out[j, plane - HALO, row : row + TILE, :] = total + (time_step / 6) * rates[j]

    over_rates(fourth, coefs, edge, 1, two, beyond)
    over_rates(fourth, coefs, 3 - core(), OWN - 1, two)


def hold_kernel(value, after, out, sems):
    del after
    run_copies([(value, out)], sems)


def residual_kernel(vec, own, previous, *rest):
    out, held, sems = rest[-3:]
    copies = []
    for j in range(2):
        held[2 * j : 2 * j + 2] = own[2 * j : 2 * j + 2] - previous[2 * j : 2 * j + 2]
        copies.append(pltpu.make_async_copy(held.at[2 * j : 2 * j + 2], out.at[0, vec, 2 * j : 2 * j + 2], sems.at[j]))
        copies[-1].start()
    for copy in copies:
        copy.wait()


def shards(state, flow):
    rows, lanes = state.shape[-2:]
    slabs, segs = lax.axis_size("slab"), lax.axis_size("seg")
    near_pairs = [(i, i ^ 1) for i in range(slabs)]
    seg_pairs = [(i, (i + 1) % segs) for i in range(segs)]
    far_pairs = []
    for seg in range(segs):
        for slab in range(slabs):
            if slab in (0, slabs - 1):
                to = (seg ^ 2) * slabs + slab
            else:
                to = seg * slabs + (slab + 1 if slab % 2 else slab - 1)
            far_pairs.append((seg * slabs + slab, to))

    def far_swap(value):
        return lax.ppermute(value, ("seg", "slab"), far_pairs)

    def near_swap(value):
        return lax.ppermute(value, "slab", near_pairs)

    def planes(fields, count):
        return jax.ShapeDtypeStruct((fields, count, rows, lanes), F32)

    def scratch(fields, count):
        return pltpu.VMEM((fields, count, rows, lanes), F32)

    anywhere = pl.BlockSpec(memory_space=pl.ANY)
    vmem = pl.BlockSpec(memory_space=pltpu.VMEM)
    cost = pl.CostEstimate(flops=30_000_000, bytes_accessed=6_000_000, transcendentals=0)
    params = pltpu.CompilerParams(vmem_limit_bytes=16 * 1024 * 1024)

    def call(kernel, name, in_specs, out_shape, scratch_shapes, copies, **options):
        outs = out_shape if isinstance(out_shape, tuple) else (out_shape,)
        return pl.pallas_call(
            kernel,
            out_shape=out_shape,
            in_specs=in_specs,
            out_specs=options.pop("out_specs", (vmem,) * len(outs) if isinstance(out_shape, tuple) else vmem),
            scratch_shapes=scratch_shapes + [pltpu.SemaphoreType.DMA((copies,))],
            compiler_params=params,
            name=name,
            **options,
        )

    state_there = pltpu.with_memory_space_constraint(state, pltpu.HBM)
    flow_there = pltpu.with_memory_space_constraint(flow, pltpu.HBM)
    far_a, near = call(
        pack_kernel,
        "pack",
        [anywhere] * 2,
        (scratch(11, 1), scratch(11, HALO)),
        [scratch(4, 3), scratch(3, 3), scratch(COEFS, 1)],
        5,
    )(state_there, flow_there)
    near = near_swap(near)
    far_a = far_swap(far_a)

    coefs, own0, own1, *inner0 = call(
        inner_0_kernel,
        "inner_0",
        [anywhere] * 3,
        (planes(COEFS, COEF_PLANES), planes(4, OWN), planes(4, OWN), planes(4, OWN), planes(4, HALO), planes(4, HALO)),
        [scratch(4, WIDE), scratch(3, WIDE), scratch(4, WIDE)],
        6,
        cost_estimate=cost,
    )(state_there, flow_there, near)
    *inner1, far_b, near_mid = call(
        inner_1_kernel,
        "inner_1",
        [anywhere, anywhere, vmem, anywhere],
        (planes(4, OWN), planes(4, HALO), planes(4, HALO), planes(8, 1), planes(8, HALO)),
        [scratch(4, WIDE), scratch(4, WIDE)],
        3,
        cost_estimate=cost,
    )(own1, near, coefs, inner0[1])
    far_b = far_swap(far_b)
    near_mid = near_swap(near_mid)

    def first(vec, own, far_at, far_q, ready, *after):
        return call(
            functools.partial(first_kernel, far_at),
            f"first_{vec}",
            [anywhere, vmem] + [anywhere] * 7,
            (planes(4, OWN), planes(4, OWN), planes(8, 1)),
            [scratch(4, WIDE), scratch(4, WIDE), scratch(4, WIDE), scratch(4, 1), scratch(3, 1), scratch(3, 1)],
            7,
            cost_estimate=cost,
        )(own, coefs, far_a, far_q, *ready, *after)

    def second(vec, own, near_at, far_at, far_q, mid, part, far_mid, after):
        return call(
            functools.partial(second_kernel, near_at, far_at),
            f"second_{vec}",
            [anywhere, vmem] + [anywhere] * 4 + [vmem] + [anywhere] * 3,
            planes(4, OWN),
            [scratch(4, WIDE), scratch(4, WIDE), scratch(4, WIDE), scratch(4, 1), scratch(3, 1), scratch(3, 1)],
            8,
            cost_estimate=cost,
        )(own, coefs, near, far_a, far_q, mid, part, far_mid, near_mid, after)

    def residual(vec, own, previous, *buffer):
        return call(
            functools.partial(residual_kernel, vec),
            f"residual_{vec}",
            [vmem, vmem] + [anywhere] * vec,
            pltpu.HBM(state.shape, F32),
            [scratch(4, OWN)],
            4,
            out_specs=anywhere,
            input_output_aliases={2: 0} if vec else {},
        )(own, previous, *buffer)

    mid0, part0, far0 = first(0, own0, 3, far_a, inner0, inner1[1], inner1[1])
    far0 = far_swap(far0)
    mid1, part1, far1 = first(1, own1, 0, far_b, inner1, mid0, mid0)
    far1 = far_swap(far1)
    out0 = second(0, own0, 3, 3, far_a, mid0, part0, far0, mid1)
    held0 = call(hold_kernel, "hold", [anywhere] * 2, scratch(4, OWN), [], 1)(out0, far1)
    prev0 = lax.ppermute(held0, "seg", seg_pairs)
    out1 = second(1, own1, 7, 0, far_b, mid1, part1, far1, out0)
    prev1 = lax.ppermute(out1, "seg", seg_pairs)
    advanced = jnp.stack([out0, out1])[None]
    return advanced, residual(1, own1, prev1, residual(0, own0, prev0))


def solution(mesh):
    return jax.shard_map(
        shards,
        mesh=mesh,
        in_specs=(P("seg", None, None, "slab", None, None), P("seg", None, "slab", None, None)),
        out_specs=(
            P("seg", None, None, "slab", None, None),
            P("seg", None, None, "slab", None, None),
        ),
        check_vma=False,
    )
```
